768 devices in a mesh: group: 48 (over x, z), row: 8 (over y), col: 2 (over core).
Axes of the slice: x: 4, y: 8, z: 12, core: 2. Of those that a mesh axis runs over, the one named last changes fastest.
Arguments:
- activations: bfloat16 [12288, 8192], P('group', ('row', 'col')), may hold values from -6 to 6
- base_weight_codes: bfloat16 [8192, 8192], P('row', 'col'), may hold values from -6 to 6, as said below
- block_scale_exponents: int32 [256, 8192], P('row', 'col'), may hold values from -10 to -7
- adapter_down_weight: float32 [192, 8192, 64], P('group', ('row', 'col')), may hold values from -0.0625 to 0.0625
- adapter_up_weight: float32 [192, 64, 2, 8, 512], P('group', None, 'col', 'row'), may hold values from -0.75 to 0.75
- row_adapter_index: int32 [12288], P('group'), may hold values from 0 to 191, as said below
- adapter_storage_slot: int32 [192], replicated, may hold values from 0 to 191, as said below
Outputs:
- projected_layer_output: bfloat16 [12288, 2, 8, 512], P('group', 'col', 'row')
The draws below stay inside these ranges and needn't reach their ends.
Inputs may be any that keep to these rules, and one draw needn't show every extreme that they name: `row_adapter_index`: every row of a group names an adapter; among the 256 rows of any one group, at most 12 name adapters whose slots lie in any one group's slots (slot // 4), and in every draw some group's slots receive exactly 12 rows from every group. A permutation: adapter a is stored in slot adapter_storage_slot[a], held by group adapter_storage_slot[a] // 4. `base_weight_codes`: each entry is one of the values 0, 0.5, 1, 1.5, 2, 3, 4, 6 or their negatives.
All inputs are finite; a program needn't handle non-finite values.
Results may differ from the reference program's by a relative error of at most 0.017.
Values may be sent and summed in bfloat16 or wider, within the bound.
A program may use at most 64 MiB of HBM per device.

```python
import math
import jax
import jax.numpy as jnp
from jax import lax

MODEL_WIDTH = 8192
ADAPTER_RANK = 64
ROWS_G = 256
AD_G = 4
ADAPTER_COUNT = 192
REQUEST_ROWS = 12288
CAP = 12
FEATURE_BLOCK = 512
N_GROUP = 48
N_ROW = 8
N_COL = 2


def routing(key):
    storage_slots = jax.random.permutation(jax.random.fold_in(key, 11), ADAPTER_COUNT).astype(jnp.int32)
    hot_group = jax.random.randint(jax.random.fold_in(key, 12), (), 0, N_GROUP)
    positions_all = N_GROUP * CAP

    def one_group(group_key):
        scores = jax.random.permutation(group_key, positions_all).astype(jnp.int32)
        owner_of = jnp.arange(positions_all, dtype=jnp.int32) // CAP
        scores = scores + jnp.where(owner_of == hot_group, positions_all, 0).astype(jnp.int32)
        unused, picked = lax.top_k(scores, ROWS_G)
        owners = (picked // CAP).astype(jnp.int32)
        shuffle = jax.random.permutation(jax.random.fold_in(group_key, 1), ROWS_G)
        owners = owners[shuffle]
        local_index = jax.random.randint(jax.random.fold_in(group_key, 2), (ROWS_G,), 0, AD_G)
        return (owners * AD_G + local_index).astype(jnp.int32)
    group_keys = jax.random.split(jax.random.fold_in(key, 13), N_GROUP)
    row_slots = jax.vmap(one_group)(group_keys).reshape(REQUEST_ROWS)
    inverse = jnp.argsort(storage_slots).astype(jnp.int32)
    return (inverse[row_slots].astype(jnp.int32), storage_slots)


def draw_row_adapter_index(key, part):
    ids_drawn, slots_drawn = routing(key)
    return ids_drawn


def draw_adapter_storage_slot(key, part):
    ids_drawn, slots_drawn = routing(key)
    return slots_drawn


def draw_base_weight_codes(key, part):
    key = jax.random.fold_in(key, 5)
    code_index = jax.random.randint(key, (MODEL_WIDTH, MODEL_WIDTH), 0, 16)
    code_values = jnp.array([0.0, 0.5, 1.0, 1.5, 2.0, 3.0, 4.0, 6.0, -0.0, -0.5, -1.0, -1.5, -2.0, -3.0, -4.0, -6.0], jnp.float32)
    return code_values[code_index].astype(jnp.bfloat16)


def plant(drawn, stream_key, least, high):
    place = [jax.random.randint(jax.random.fold_in(stream_key, axis), (), 0, length) for axis, length in enumerate(drawn.shape)]
    longest = drawn.shape.index(max(drawn.shape))
    next_to = place[:longest] + [(place[longest] + 1) % drawn.shape[longest]] + place[longest + 1:]
    return drawn.at[tuple(place)].set(least).at[tuple(next_to)].set(high)


def block_levels(key, dims, pieces, low, top_value):
    def one(axis_at, parts):
        draws = jax.random.uniform(jax.random.fold_in(jax.random.fold_in(key, 6), axis_at), (parts,), jnp.float32, low / len(pieces), top_value / len(pieces))
        return jnp.repeat(jnp.exp(draws), dims[axis_at] // parts).reshape((-1,) + (1,) * (len(dims) - axis_at - 1))

    level = one(*pieces[0])
    for cut in pieces[1:]:
        level = level * one(*cut)
    return level


def noise(stream_key, shape, scale, most, cuts=(), held_as=jnp.bfloat16):
    values = jax.random.normal(stream_key, shape, jnp.float32) * scale
    if len(cuts) > 0:
        values = block_levels(stream_key, shape, cuts, -0.22, 0.18) * values
    return jnp.clip(values, min=-most, max=most).astype(held_as)


def setup_inputs(seed: int = 0) -> dict:
    streams_of = jax.random.split(jax.random.key(seed), 8)
    activations = noise(streams_of[0], (REQUEST_ROWS, MODEL_WIDTH), 1.0, 6.0, ((0, 48), (1, 16)))
    base_weight_codes = draw_base_weight_codes(jax.random.fold_in(streams_of[7], 71), 0)
    block_scale_exponents = plant(jax.random.randint(streams_of[2], (MODEL_WIDTH // 32, MODEL_WIDTH), -10, -6), jax.random.fold_in(streams_of[2], 1), -10, (-6) - 1).astype(jnp.int32)
    adapter_down_weight = noise(streams_of[3], (ADAPTER_COUNT, MODEL_WIDTH, ADAPTER_RANK), MODEL_WIDTH ** -0.5, 0.0625, ((0, 48), (1, 16)), jnp.float32)
    adapter_up_weight = noise(streams_of[4], (ADAPTER_COUNT, ADAPTER_RANK, N_COL, N_ROW, FEATURE_BLOCK), ADAPTER_RANK ** -0.5, 0.75, ((0, 48), (2, 2), (3, 8)), jnp.float32)
    row_adapter_index = draw_row_adapter_index(jax.random.fold_in(streams_of[7], 71), 0)
    adapter_storage_slot = draw_adapter_storage_slot(jax.random.fold_in(streams_of[7], 71), 0)
    return {"activations": activations, "base_weight_codes": base_weight_codes, "block_scale_exponents": block_scale_exponents, "adapter_down_weight": adapter_down_weight, "adapter_up_weight": adapter_up_weight, "row_adapter_index": row_adapter_index, "adapter_storage_slot": adapter_storage_slot}


def reference(activations, base_weight_codes, block_scale_exponents, adapter_down_weight, adapter_up_weight, row_adapter_index, adapter_storage_slot):
    scaling = jnp.exp2(block_scale_exponents.astype(jnp.float32))
    weight = (base_weight_codes.astype(jnp.float32).reshape(MODEL_WIDTH // 32, 32, MODEL_WIDTH) * scaling[:, None, :]).reshape(MODEL_WIDTH, MODEL_WIDTH).astype(jnp.bfloat16)
    base_projection_output = jnp.dot(activations, weight, preferred_element_type=jnp.float32)
    storage_slot_index = adapter_storage_slot[row_adapter_index].astype(jnp.int32)
    up_weight_flat = adapter_up_weight.reshape(ADAPTER_COUNT, ADAPTER_RANK, MODEL_WIDTH)
    row_block_index = math.gcd(REQUEST_ROWS, 64)

    def single_block(block_args):
        row_slice, storage_slots = block_args
        down_projected_rows = adapter_down_weight[storage_slots]
        low_rank = jnp.einsum('rd,rdk->rk', row_slice.astype(jnp.float32), down_projected_rows, precision=lax.Precision.HIGHEST)
        up_rows = up_weight_flat[storage_slots]
        return jnp.einsum('rk,rkf->rf', low_rank, up_rows, precision=lax.Precision.HIGHEST).astype(jnp.bfloat16)

    adapter_delta = lax.map(single_block, (activations.reshape(-1, row_block_index, MODEL_WIDTH), storage_slot_index.reshape(-1, row_block_index))).reshape(REQUEST_ROWS, MODEL_WIDTH)
    projected_layer_output = (base_projection_output + adapter_delta.astype(jnp.float32)).astype(jnp.bfloat16)
    return projected_layer_output.reshape(REQUEST_ROWS, N_COL, N_ROW, MODEL_WIDTH // (N_COL * N_ROW))
```

```python
import functools

import jax
import jax.numpy as jnp
from jax import lax
from jax.experimental import pallas as pl
from jax.experimental.pallas import tpu as pltpu
from jax.sharding import PartitionSpec as P

MESH = pl.DeviceIdType.MESH
F32 = jnp.float32
BF16 = jnp.bfloat16
I32 = jnp.int32

NX = 4
NZ = 12
NROW = 8
NFLAT = 16
ROWS = 256
FEAT = 512
BLK = 48
RANK = 64
AD = 4
SLAB_W = NX * AD * RANK

ORDER = (0, 1, 11, 2, 10, 3, 9, 4, 8, 5, 7, 6)
CHUNKS = ((0, 12),)


def kernel(
    act_h,
    codes_h,
    scl_h,
    down_h,
    up_h,
    ids_ref,
    tab_ref,
    out_ref,
    a_all,
    w_v,
    scl_v,
    down_v,
    up_v,
    tab_v,
    choose,
    xs,
    xr,
    ids_s,
    ids_r,
    d_all,
    u_all,
    part,
    sp,
    sm,
    rp,
    rm,
    low_s,
    red,
    low_full,
    back_s,
    back_r,
    acc,
    load_sem,
    w_sem,
    a_sem,
    x_send,
    x_recv,
    i_send,
    i_recv,
    ad_send,
    ad_recv,
    rs_send,
    rs_recv,
    low_send,
    red_recv,
    full_send,
    full_recv,
    b_send,
    b_recv,
):
    g = lax.axis_index("group")
    r = lax.axis_index("row")
    c = lax.axis_index("col")
    x = g // NZ
    z = g % NZ
    flat = 2 * r + c

    def at_z(offset):
        return (x * NZ + (z + offset + NZ) % NZ, r, c)

    def at_x(offset):
        return (((x + offset + NX) % NX) * NZ + z, r, c)

    def at_row(offset):
        return (g, (r + offset + NROW) % NROW, c)

    def block_of(i):
        return (r + 4 + ((i + 1) // 2) * (1 - 2 * (i % 2)) + NROW) % NROW

    load_a = pltpu.make_async_copy(act_h, a_all.at[c], load_sem.at[0])
    load_s = pltpu.make_async_copy(scl_h, scl_v, load_sem.at[1])
    load_d = pltpu.make_async_copy(down_h, down_v, load_sem.at[2])
    load_u = pltpu.make_async_copy(up_h, up_v, load_sem.at[3])

    def load_w(i):
        columns = pl.ds(pl.multiple_of(block_of(i) * FEAT, FEAT), FEAT)
        return pltpu.make_async_copy(codes_h.at[:, columns], w_v.at[i], w_sem.at[i])

    load_a.start()
    load_w(0).start()
    load_s.start()
    load_d.start()
    for i in range(1, NROW):
        load_w(i).start()
    load_u.start()

    barrier = pltpu.get_barrier_semaphore()
    peers = [at_z(o) for o in range(1, NZ)]
    peers += [at_x(o) for o in range(1, NX)]
    for device in peers:
        pl.semaphore_signal(barrier, inc=1, device_id=device, device_id_type=MESH)

    def greet(i, carry):
        pl.semaphore_signal(
            barrier,
            inc=1,
            device_id=(g, (r + i // 2) % NROW, (c + i % 2) % 2),
            device_id_type=MESH,
        )
        return carry

    lax.fori_loop(1, NFLAT, greet, 0)

    tab_v[...] = jnp.zeros(tab_v.shape, F32)
    tab_v[:, : tab_ref.shape[1]] = tab_ref[...].astype(F32)
    ids = ids_ref[...]
    match = (lax.broadcasted_iota(I32, (256, ROWS), 0) == ids).astype(F32).astype(BF16)
    slots = jnp.dot(
        jnp.broadcast_to(tab_v[...], (8, 256)).astype(BF16), match, preferred_element_type=F32
    ).astype(I32)
    owner = slots >> 2
    owner_x = (
        (owner >= NZ).astype(I32) + (owner >= 2 * NZ).astype(I32) + (owner >= 3 * NZ).astype(I32)
    )
    away = z - (owner - NZ * owner_x)
    away = jnp.where(away < 0, away + NZ, away)
    place = jnp.zeros_like(away)
    for q, o in enumerate(ORDER):
        place = jnp.where(away == o, q, place)
    adapter = (owner_x * AD + (slots & 3) + 1).astype(F32).astype(BF16)
    sent_to = lax.broadcasted_iota(I32, (16, ROWS), 0) == place[0:1]
    before = (
        lax.broadcasted_iota(I32, (ROWS, ROWS), 0) < lax.broadcasted_iota(I32, (ROWS, ROWS), 1)
    )
    prefix = jnp.dot(
        sent_to.astype(F32).astype(BF16),
        before.astype(F32).astype(BF16),
        preferred_element_type=F32,
    )
    position = jnp.sum(jnp.where(sent_to, prefix, 0.0), axis=0, keepdims=True).astype(I32)
    target = place[0:1] * BLK + position
    choose[...] = (
        (lax.broadcasted_iota(I32, (NZ * BLK, ROWS), 0) == target).astype(F32).astype(BF16)
    )
    ids_s[...] = jnp.zeros(ids_s.shape, F32)
    for q in range(NZ):
        row = lax.dot_general(
            adapter,
            choose[q * BLK : (q + 1) * BLK, :],
            (((1,), (1,)), ((), ())),
            preferred_element_type=F32,
        )
        ids_s[q, :, 0:BLK] = row[0:1]
    ids_r[0] = ids_s[0]
    load_a.wait()
    xs[...] = jnp.dot(choose[...], a_all[c], preferred_element_type=F32).astype(BF16)
    xr[0:BLK] = xs[0:BLK]

    pl.semaphore_wait(barrier, len(peers) + NFLAT - 1)

    def send_rows(q):
        rows = pl.ds(q * BLK, BLK)
        return pltpu.make_async_remote_copy(
            src_ref=xs.at[rows],
            dst_ref=xr.at[rows],
            send_sem=x_send.at[q],
            recv_sem=x_recv.at[q],
            device_id=at_z(-ORDER[q]),
            device_id_type=MESH,
        )

    def send_ids(q):
        return pltpu.make_async_remote_copy(
            src_ref=ids_s.at[q],
            dst_ref=ids_r.at[q],
            send_sem=i_send.at[q],
            recv_sem=i_recv.at[q],
            device_id=at_z(-ORDER[q]),
            device_id_type=MESH,
        )

    def send_back(q):
        rows = pl.ds(q * BLK, BLK)
        return pltpu.make_async_remote_copy(
            src_ref=back_s.at[rows],
            dst_ref=back_r.at[rows],
            send_sem=b_send.at[q],
            recv_sem=b_recv.at[q],
            device_id=at_z(ORDER[q]),
            device_id_type=MESH,
        )

    swap_a = pltpu.make_async_remote_copy(
        src_ref=a_all.at[c],
        dst_ref=a_all.at[c],
        send_sem=a_sem.at[0],
        recv_sem=a_sem.at[1],
        device_id=(g, r, 1 - c),
        device_id_type=MESH,
    )
    take_a = pltpu.make_async_remote_copy(
        src_ref=a_all.at[1 - c],
        dst_ref=a_all.at[1 - c],
        send_sem=a_sem.at[0],
        recv_sem=a_sem.at[1],
        device_id=(g, r, 1 - c),
        device_id_type=MESH,
    )
    swap_a.start()
    for q in range(1, NZ):
        send_ids(q).start()
        send_rows(q).start()

    def share(buffer, base, kind):
        half = AD * RANK // 2
        where = {
            "right": (x, pl.ds(0, 2 * half), 1),
            "left": (x, pl.ds(0, 2 * half), -1),
            "far_right": ((x + NX - 1) % NX, pl.ds(0, half), 1),
            "far_left": ((x + 1) % NX, pl.ds(half, half), -1),
        }
        at, rows, step = where[kind]
        n = base + ("right", "left", "far_right", "far_left").index(kind)
        return pltpu.make_async_remote_copy(
            src_ref=buffer.at[at, rows],
            dst_ref=buffer.at[at, rows],
            send_sem=ad_send.at[n],
            recv_sem=ad_recv.at[n],
            device_id=at_x(step),
            device_id_type=MESH,
        )

    def arrived(buffer, base, kind):
        half = AD * RANK // 2
        where = {
            "right": ((x + NX - 1) % NX, pl.ds(0, 2 * half)),
            "left": ((x + 1) % NX, pl.ds(0, 2 * half)),
            "far_right": ((x + 2) % NX, pl.ds(0, half)),
            "far_left": ((x + 2) % NX, pl.ds(half, half)),
        }
        at, rows = where[kind]
        n = base + ("right", "left", "far_right", "far_left").index(kind)
        return pltpu.make_async_remote_copy(
            src_ref=buffer.at[at, rows],
            dst_ref=buffer.at[at, rows],
            send_sem=ad_send.at[n],
            recv_sem=ad_recv.at[n],
            device_id=at_x(1),
            device_id_type=MESH,
        )

    load_d.wait()
    d_all[x] = down_v[...].astype(BF16)
    share(d_all, 0, "right").start()
    share(d_all, 0, "left").start()

    half_rows = (pl.ds(0, ROWS // 2), pl.ds(ROWS // 2, ROWS // 2))

    def ring(direction, step, half):
        source, landing, way = ((sp, rp, 1), (sm, rm, -1))[direction]
        return pltpu.make_async_remote_copy(
            src_ref=source.at[step, half_rows[half]],
            dst_ref=landing.at[step, half_rows[half]],
            send_sem=rs_send.at[direction, step, half],
            recv_sem=rs_recv.at[direction, step, half],
            device_id=at_row(way),
            device_id_type=MESH,
        )

    load_s.wait()
    take_a.wait_recv()

    def base_block(i, carry):
        load_w(i).wait()
        columns = pl.ds(pl.multiple_of(block_of(i) * FEAT, FEAT), FEAT)
        scale = jnp.exp2(scl_v[:, columns].astype(F32)).astype(BF16)
        weight = (w_v[i].reshape(32, 32, FEAT) * scale[:, None, :]).reshape(2 * FEAT, FEAT)
        value = jnp.dot(a_all[0], weight[:FEAT], preferred_element_type=F32)
        value += jnp.dot(a_all[1], weight[FEAT:], preferred_element_type=F32)
        part[i] = value

        @pl.when(i == 0)
        def _():
            sp[0, half_rows[0]] = part[0, half_rows[0]].astype(BF16)
            ring(0, 0, 0).start()
            sm[0, half_rows[1]] = part[0, half_rows[1]].astype(BF16)
            ring(1, 0, 1).start()

        @pl.when(i == 1)
        def _():
            sp[1, half_rows[1]] = part[1, half_rows[1]].astype(BF16)
            ring(0, 1, 1).start()

        @pl.when(i == 2)
        def _():
            sm[1, half_rows[0]] = part[2, half_rows[0]].astype(BF16)
            ring(1, 1, 0).start()

        return carry

    lax.fori_loop(0, NROW, base_block, 0)

    load_u.wait()
    for q in range(FEAT // 128):
        u_all[x, :, q * 128 : (q + 1) * 128] = up_v[pl.ds(q, AD * RANK, stride=4), :].astype(BF16)
    arrived(d_all, 0, "right").wait_recv()
    share(d_all, 0, "far_right").start()
    arrived(d_all, 0, "left").wait_recv()
    share(d_all, 0, "far_left").start()
    share(u_all, 4, "right").start()
    share(u_all, 4, "left").start()

    def ring_step(direction, step, half):
        ring(direction, step - 1, half).wait_recv()
        source, landing, _ = ((sp, rp, 1), (sm, rm, -1))[direction]
        rows = half_rows[half]
        own = part[2 * step - 1 + direction, rows]
        source[step, rows] = (landing[step - 1, rows].astype(F32) + own).astype(BF16)
        ring(direction, step, half).start()

    ring_step(0, 1, 0)
    ring_step(1, 1, 1)
    for step in (2, 3):
        ring_step(0, step, 1)
        ring_step(1, step, 0)
        ring_step(0, step, 0)
        ring_step(1, step, 1)
        if step == 2:
            arrived(u_all, 4, "right").wait_recv()
            share(u_all, 4, "far_right").start()
            arrived(u_all, 4, "left").wait_recv()
            share(u_all, 4, "far_left").start()

    lane = lax.broadcasted_iota(I32, (BLK // 2, 128), 1)
    eye = lax.broadcasted_iota(I32, (BLK, 128), 0) == lax.broadcasted_iota(I32, (BLK, 128), 1)
    lane_adapter = (lax.broadcasted_iota(I32, (BLK, SLAB_W), 1) // RANK + 1).astype(F32)

    def adapter_mask(q):
        wanted = jnp.sum(jnp.where(eye, ids_r[q], 0.0), axis=1, keepdims=True)
        return lane_adapter == wanted

    def to_reducer(q):
        return pltpu.make_async_remote_copy(
            src_ref=low_s.at[q],
            dst_ref=red.at[flat],
            send_sem=low_send.at[q],
            recv_sem=red_recv.at[flat],
            device_id=(g, q // 2, q % 2),
            device_id_type=MESH,
        )

    def from_device(i):
        return pltpu.make_async_remote_copy(
            src_ref=red.at[i],
            dst_ref=red.at[i],
            send_sem=low_send.at[0],
            recv_sem=red_recv.at[i],
            device_id=(g, (r + 1) % NROW, c),
            device_id_type=MESH,
        )

    def to_all(q, i):
        return pltpu.make_async_remote_copy(
            src_ref=low_full.at[q],
            dst_ref=low_full.at[q],
            send_sem=full_send.at[i],
            recv_sem=full_recv.at[q],
            device_id=(g, (r + i // 2) % NROW, (c + i % 2) % 2),
            device_id_type=MESH,
        )

    for first, last in CHUNKS:
        rows = slice(first * BLK, last * BLK)
        for q in range(first, last):
            if q > 0:
                send_ids(q).wait_recv()
                send_rows(q).wait_recv()
        if first == 0:
            arrived(d_all, 0, "far_right").wait_recv()
            arrived(d_all, 0, "far_left").wait_recv()
        projected = lax.dot_general(
            xr[rows],
            d_all[...].reshape(SLAB_W, FEAT),
            (((1,), (1,)), ((), ())),
            preferred_element_type=F32,
        )
        for q in range(first, last):
            block = projected[(q - first) * BLK : (q - first + 1) * BLK]
            block = jnp.where(adapter_mask(q), block, 0.0)
            folded = block[:, 0:128]
            for k in range(1, SLAB_W // 128):
                folded += block[:, k * 128 : (k + 1) * 128]
            folded += pltpu.roll(folded, RANK, 1)
            low_s[q] = jnp.where(lane < RANK, folded[: BLK // 2], folded[BLK // 2 :])

            @pl.when(flat != q)
            def _():
                to_reducer(q).start()

            @pl.when(flat == q)
            def _():
                red[flat] = low_s[q]

        for q in range(first, last):

            @pl.when(flat == q)
            def _():
                for i in range(NFLAT):
                    if i != q:
                        from_device(i).wait_recv()
                total = red[0]
                for i in range(1, NFLAT):
                    total += red[i]
                low_full[q] = total

                def hand_out(i, carry):
                    to_all(q, i).start()
                    return carry

                lax.fori_loop(1, NFLAT, hand_out, 0)

        if first == 0:
            arrived(u_all, 4, "far_right").wait_recv()
            arrived(u_all, 4, "far_left").wait_recv()
        spread = []
        for q in range(first, last):

            @pl.when(flat != q)
            def _():
                to_all(q, 1).wait_recv()

            packed = low_full[q]
            turned = pltpu.roll(packed, RANK, 1)
            both = jnp.concatenate(
                [jnp.where(lane < RANK, packed, turned), jnp.where(lane < RANK, turned, packed)],
                axis=0,
            )
            wide = jnp.concatenate([both] * (SLAB_W // 128), axis=1)
            spread.append(jnp.where(adapter_mask(q), wide, 0.0).astype(BF16))
        delta = jnp.dot(
            jnp.concatenate(spread, axis=0),
            u_all[...].reshape(SLAB_W, FEAT),
            preferred_element_type=F32,
        ).astype(BF16)
        back_s[rows] = delta
        for q in range(first, last):
            if q > 0:
                send_back(q).start()
            else:
                back_r[0:BLK] = delta[0:BLK]

    for half in (1, 0):
        ring(0, 3, half).wait_recv()
        ring(1, 3, 1 - half).wait_recv()
    acc[...] = part[7] + (rp[3].astype(F32) + rm[3].astype(F32))

    for q in range(1, NZ):
        send_back(q).wait_recv()
    added = lax.dot_general(
        choose[...], back_r[...], (((0,), (0,)), ((), ())), preferred_element_type=F32
    )
    out_ref[...] = (acc[...] + added).astype(BF16)

    swap_a.wait_send()
    for q in range(1, NZ):
        send_ids(q).wait_send()
        send_rows(q).wait_send()
        send_back(q).wait_send()
    for buffer, base in ((d_all, 0), (u_all, 4)):
        for kind in ("right", "left", "far_right", "far_left"):
            share(buffer, base, kind).wait_send()
    for direction in (0, 1):
        ring(direction, 0, direction).wait_send()
        for step in (1, 2, 3):
            for half in (0, 1):
                ring(direction, step, half).wait_send()
    for q in range(NZ):

        @pl.when(flat != q)
        def _():
            to_reducer(q).wait_send()

        @pl.when(flat == q)
        def _():
            def left(i, carry):
                to_all(q, i).wait_send()
                return carry

            lax.fori_loop(1, NFLAT, left, 0)


def per_device(
    activations,
    base_weight_codes,
    block_scale_exponents,
    adapter_down_weight,
    adapter_up_weight,
    row_adapter_index,
    adapter_storage_slot,
):
    down = jnp.transpose(adapter_down_weight, (0, 2, 1)).reshape(AD * RANK, FEAT)
    up = adapter_up_weight.reshape(AD * RANK * FEAT // 128, 128)
    hbm = pl.BlockSpec(memory_space=pl.ANY)
    vmem = pl.BlockSpec(memory_space=pltpu.VMEM)
    dma = pltpu.SemaphoreType.DMA
    padded = NZ * BLK
    out = pl.pallas_call(
        kernel,
        out_shape=jax.ShapeDtypeStruct((ROWS, FEAT), BF16),
        in_specs=[hbm] * 5 + [vmem] * 2,
        out_specs=vmem,
        scratch_shapes=[
            pltpu.VMEM((2, ROWS, FEAT), BF16),
            pltpu.VMEM((NROW, 2 * FEAT, FEAT), BF16),
            pltpu.VMEM((32, NROW * FEAT), I32),
            pltpu.VMEM((AD * RANK, FEAT), F32),
            pltpu.VMEM((AD * RANK * FEAT // 128, 128), F32),
            pltpu.VMEM((1, 256), F32),
            pltpu.VMEM((padded, ROWS), BF16),
            pltpu.VMEM((padded, FEAT), BF16),
            pltpu.VMEM((padded, FEAT), BF16),
            pltpu.VMEM((NZ, 1, 128), F32),
            pltpu.VMEM((NZ, 1, 128), F32),
            pltpu.VMEM((NX, AD * RANK, FEAT), BF16),
            pltpu.VMEM((NX, AD * RANK, FEAT), BF16),
            pltpu.VMEM((NROW, ROWS, FEAT), F32),
            pltpu.VMEM((4, ROWS, FEAT), BF16),
            pltpu.VMEM((4, ROWS, FEAT), BF16),
            pltpu.VMEM((4, ROWS, FEAT), BF16),
            pltpu.VMEM((4, ROWS, FEAT), BF16),
            pltpu.VMEM((NZ, BLK // 2, 128), F32),
            pltpu.VMEM((NFLAT, BLK // 2, 128), F32),
            pltpu.VMEM((NZ, BLK // 2, 128), F32),
            pltpu.VMEM((padded, FEAT), BF16),
            pltpu.VMEM((padded, FEAT), BF16),
            pltpu.VMEM((ROWS, FEAT), F32),
            dma((4,)),
            dma((NROW,)),
            dma((2,)),
            dma((NZ,)),
            dma((NZ,)),
            dma((NZ,)),
            dma((NZ,)),
            dma((8,)),
            dma((8,)),
            dma((2, 4, 2)),
            dma((2, 4, 2)),
            dma((NZ,)),
            dma((NFLAT,)),
            dma((NFLAT,)),
            dma((NZ,)),
            dma((NZ,)),
            dma((NZ,)),
        ],
        compiler_params=pltpu.CompilerParams(
            collective_id=0, has_side_effects=True, vmem_limit_bytes=56 * 1024 * 1024
        ),
        cost_estimate=pl.CostEstimate(
            flops=2 * ROWS * 2 * FEAT * NROW * FEAT, bytes_accessed=11 << 20, transcendentals=0
        ),
        name="projection",
    )(
        activations,
        base_weight_codes,
        block_scale_exponents,
        down,
        up,
        row_adapter_index.reshape(1, ROWS),
        adapter_storage_slot.reshape(1, -1),
    )
    return out.reshape(ROWS, 1, 1, FEAT)


def solution(mesh):
    return jax.shard_map(
        per_device,
        mesh=mesh,
        in_specs=(
            P("group", ("row", "col")),
            P("row", "col"),
            P("row", "col"),
            P("group", ("row", "col"), None),
            P("group", None, "col", "row", None),
            P("group"),
            P(),
        ),
        out_specs=P("group", "col", "row", None),
        check_vma=False,
    )
```

```python
import functools

import jax
import jax.numpy as jnp
from jax import lax
from jax.experimental import pallas as pl
from jax.experimental.pallas import tpu as pltpu
from jax.sharding import PartitionSpec as P

MESH = pl.DeviceIdType.MESH
F32 = jnp.float32
BF16 = jnp.bfloat16
I32 = jnp.int32

NX = 4
NZ = 12
NROW = 8
NFLAT = 16
ROWS = 256
FEAT = 512
BLK = 48
RANK = 64
AD = 4
SLAB_W = NX * AD * RANK

CHUNKS = ((0, 4), (4, 8), (8, 12))


def kernel(
    act_h,
    codes_h,
    scl_h,
    down_h,
    up_h,
    ids_ref,
    tab_ref,
    out_ref,
    a_all,
    w_v,
    scl_v,
    down_v,
    up_v,
    tab_v,
    choose,
    xs,
    xr,
    ids_s,
    ids_r,
    d_all,
    u_all,
    part,
    sp,
    sm,
    rp,
    rm,
    low_s,
    red,
    low_full,
    back_s,
    back_r,
    acc,
    load_sem,
    w_sem,
    a_sem,
    x_send,
    x_recv,
    i_send,
    i_recv,
    ad_send,
    ad_recv,
    rs_send,
    rs_recv,
    low_send,
    red_recv,
    full_send,
    full_recv,
    b_send,
    b_recv,
    hello,
):
    g = lax.axis_index("group")
    r = lax.axis_index("row")
    c = lax.axis_index("col")
    x = g // NZ
    z = g % NZ
    flat = 2 * r + c

    def at_z(there):
        return (x * NZ + there, r, c)

    def at_x(offset):
        return (((x + offset + NX) % NX) * NZ + z, r, c)

    def at_row(offset):
        return (g, (r + offset + NROW) % NROW, c)

    def block_of(i):
        return (r + 4 + ((i + 1) // 2) * (1 - 2 * (i % 2)) + NROW) % NROW

    load_a = pltpu.make_async_copy(act_h, a_all.at[c], load_sem.at[0])
    load_s = pltpu.make_async_copy(scl_h, scl_v, load_sem.at[1])
    load_d = pltpu.make_async_copy(down_h, down_v, load_sem.at[2])
    load_u = pltpu.make_async_copy(up_h, up_v, load_sem.at[3])

    def load_w(i):
        columns = pl.ds(pl.multiple_of(block_of(i) * FEAT, FEAT), FEAT)
        return pltpu.make_async_copy(codes_h.at[:, columns], w_v.at[i], w_sem.at[i])

    load_a.start()
    load_w(0).start()
    load_s.start()
    load_d.start()
    for i in range(1, NROW):
        load_w(i).start()
    load_u.start()

    barrier = pltpu.get_barrier_semaphore()
    for o in range(1, NX):
        pl.semaphore_signal(barrier, inc=1, device_id=at_x(o), device_id_type=MESH)

    def greet_later(there, carry):
        pl.semaphore_signal(barrier, inc=1, device_id=at_z(there), device_id_type=MESH)
        return carry

    def greet(i, carry):
        pl.semaphore_signal(
            barrier,
            inc=1,
            device_id=(g, (r + i // 2) % NROW, (c + i % 2) % 2),
            device_id_type=MESH,
        )
        return carry

    lax.fori_loop(1, NFLAT, greet, 0)
    lax.fori_loop(z + 1, NZ, greet_later, 0)

    tab_v[...] = jnp.zeros(tab_v.shape, F32)
    tab_v[:, : tab_ref.shape[1]] = tab_ref[...].astype(F32)
    ids = ids_ref[...]
    match = (lax.broadcasted_iota(I32, (256, ROWS), 0) == ids).astype(F32).astype(BF16)
    slots = jnp.dot(
        jnp.broadcast_to(tab_v[...], (8, 256)).astype(BF16), match, preferred_element_type=F32
    ).astype(I32)
    owner = slots >> 2
    owner_x = (
        (owner >= NZ).astype(I32) + (owner >= 2 * NZ).astype(I32) + (owner >= 3 * NZ).astype(I32)
    )
    place = owner - NZ * owner_x
    adapter = (owner_x * AD + (slots & 3) + 1).astype(F32).astype(BF16)
    sent_to = lax.broadcasted_iota(I32, (16, ROWS), 0) == place[0:1]
    before = (
        lax.broadcasted_iota(I32, (ROWS, ROWS), 0) < lax.broadcasted_iota(I32, (ROWS, ROWS), 1)
    )
    prefix = jnp.dot(
        sent_to.astype(F32).astype(BF16),
        before.astype(F32).astype(BF16),
        preferred_element_type=F32,
    )
    position = jnp.sum(jnp.where(sent_to, prefix, 0.0), axis=0, keepdims=True).astype(I32)
    target = place[0:1] * BLK + position

    pl.semaphore_wait(barrier, NX - 1 + NFLAT - 1 + z)

    def greet_earlier(there, carry):
        pl.semaphore_signal(hello.at[z], inc=1, device_id=at_z(there), device_id_type=MESH)
        return carry

    lax.fori_loop(0, z, greet_earlier, 0)

    swap_a = pltpu.make_async_remote_copy(
        src_ref=a_all.at[c],
        dst_ref=a_all.at[c],
        send_sem=a_sem.at[0],
        recv_sem=a_sem.at[1],
        device_id=(g, r, 1 - c),
        device_id_type=MESH,
    )
    take_a = pltpu.make_async_remote_copy(
        src_ref=a_all.at[1 - c],
        dst_ref=a_all.at[1 - c],
        send_sem=a_sem.at[0],
        recv_sem=a_sem.at[1],
        device_id=(g, r, 1 - c),
        device_id_type=MESH,
    )

    def share(buffer, base, kind):
        half = AD * RANK // 2
        where = {
            "right": (x, pl.ds(0, 2 * half), 1),
            "left": (x, pl.ds(0, 2 * half), -1),
            "far_right": ((x + NX - 1) % NX, pl.ds(0, half), 1),
            "far_left": ((x + 1) % NX, pl.ds(half, half), -1),
        }
        at, rows, step = where[kind]
        n = base + ("right", "left", "far_right", "far_left").index(kind)
        return pltpu.make_async_remote_copy(
            src_ref=buffer.at[at, rows],
            dst_ref=buffer.at[at, rows],
            send_sem=ad_send.at[n],
            recv_sem=ad_recv.at[n],
            device_id=at_x(step),
            device_id_type=MESH,
        )

    def arrived(buffer, base, kind):
        half = AD * RANK // 2
        where = {
            "right": ((x + NX - 1) % NX, pl.ds(0, 2 * half)),
            "left": ((x + 1) % NX, pl.ds(0, 2 * half)),
            "far_right": ((x + 2) % NX, pl.ds(0, half)),
            "far_left": ((x + 2) % NX, pl.ds(half, half)),
        }
        at, rows = where[kind]
        n = base + ("right", "left", "far_right", "far_left").index(kind)
        return pltpu.make_async_remote_copy(
            src_ref=buffer.at[at, rows],
            dst_ref=buffer.at[at, rows],
            send_sem=ad_send.at[n],
            recv_sem=ad_recv.at[n],
            device_id=at_x(1),
            device_id_type=MESH,
        )
    load_d.wait()
    d_all[x] = down_v[...].astype(BF16)
    share(d_all, 0, "right").start()
    share(d_all, 0, "left").start()
    load_a.wait()
    swap_a.start()

    choose[...] = (
        (lax.broadcasted_iota(I32, (NZ * BLK, ROWS), 0) == target).astype(F32).astype(BF16)
    )
    ids_s[...] = jnp.zeros(ids_s.shape, F32)
    for q in range(NZ):
        row = lax.dot_general(
            adapter,
            choose[q * BLK : (q + 1) * BLK, :],
            (((1,), (1,)), ((), ())),
            preferred_element_type=F32,
        )
        ids_s[q, :, 0:BLK] = row[0:1]
    ids_r[z] = ids_s[z]
    xs[...] = (
        jnp.dot(choose[...], a_all[c], preferred_element_type=F32)
        .astype(BF16)
        .reshape(NZ, BLK, FEAT)
    )
    xr[z] = xs[z]

    def send_rows(there):
        return pltpu.make_async_remote_copy(
            src_ref=xs.at[there],
            dst_ref=xr.at[z],
            send_sem=x_send.at[there],
            recv_sem=x_recv.at[z],
            device_id=at_z(there),
            device_id_type=MESH,
        )

    def take_rows(there):
        return pltpu.make_async_remote_copy(
            src_ref=xr.at[there],
            dst_ref=xr.at[there],
            send_sem=x_send.at[there],
            recv_sem=x_recv.at[there],
            device_id=at_z(there),
            device_id_type=MESH,
        )

    def send_ids(there):
        return pltpu.make_async_remote_copy(
            src_ref=ids_s.at[there],
            dst_ref=ids_r.at[z],
            send_sem=i_send.at[there],
            recv_sem=i_recv.at[z],
            device_id=at_z(there),
            device_id_type=MESH,
        )

    def take_ids(there):
        return pltpu.make_async_remote_copy(
            src_ref=ids_r.at[there],
            dst_ref=ids_r.at[there],
            send_sem=i_send.at[there],
            recv_sem=i_recv.at[there],
            device_id=at_z(there),
            device_id_type=MESH,
        )

    def send_back(there):
        return pltpu.make_async_remote_copy(
            src_ref=back_s.at[there],
            dst_ref=back_r.at[z],
            send_sem=b_send.at[there],
            recv_sem=b_recv.at[z],
            device_id=at_z(there),
            device_id_type=MESH,
        )

    def take_back(there):
        return pltpu.make_async_remote_copy(
            src_ref=back_r.at[there],
            dst_ref=back_r.at[there],
            send_sem=b_send.at[there],
            recv_sem=b_recv.at[there],
            device_id=at_z(there),
            device_id_type=MESH,
        )

    def post_earlier(k, carry):
        there = jnp.where(k % 2 == 0, k // 2, z - 1 - k // 2)
        send_ids(there).start()
        send_rows(there).start()
        return carry

    lax.fori_loop(0, z, post_earlier, 0)

    def post_later(there):
        @pl.when(there < NZ)
        def _():
            pl.semaphore_wait(hello.at[there], 1)
            send_ids(there).start()
            send_rows(there).start()

    half_rows = (pl.ds(0, ROWS // 2), pl.ds(ROWS // 2, ROWS // 2))

    def ring(direction, step, half):
        source, landing, way = ((sp, rp, 1), (sm, rm, -1))[direction]
        return pltpu.make_async_remote_copy(
            src_ref=source.at[step, half_rows[half]],
            dst_ref=landing.at[step, half_rows[half]],
            send_sem=rs_send.at[direction, step, half],
            recv_sem=rs_recv.at[direction, step, half],
            device_id=at_row(way),
            device_id_type=MESH,
        )

    load_s.wait()
    take_a.wait_recv()

    def base_block(i, carry):
        load_w(i).wait()
        columns = pl.ds(pl.multiple_of(block_of(i) * FEAT, FEAT), FEAT)
        scale = jnp.exp2(scl_v[:, columns].astype(F32)).astype(BF16)
        weight = (w_v[i].reshape(32, 32, FEAT) * scale[:, None, :]).reshape(2 * FEAT, FEAT)
        value = jnp.dot(a_all[0], weight[:FEAT], preferred_element_type=F32)
        value += jnp.dot(a_all[1], weight[FEAT:], preferred_element_type=F32)
        part[i] = value

        @pl.when(i == 0)
        def _():
            sp[0, half_rows[0]] = part[0, half_rows[0]].astype(BF16)
            ring(0, 0, 0).start()
            sm[0, half_rows[1]] = part[0, half_rows[1]].astype(BF16)
            ring(1, 0, 1).start()

        @pl.when(i == 1)
        def _():
            sp[1, half_rows[1]] = part[1, half_rows[1]].astype(BF16)
            ring(0, 1, 1).start()

        @pl.when(i == 2)
        def _():
            sm[1, half_rows[0]] = part[2, half_rows[0]].astype(BF16)
            ring(1, 1, 0).start()

        post_later(z + 1 + i)
        return carry

    lax.fori_loop(0, NROW, base_block, 0)
    for later in range(NROW + 1, NZ):
        post_later(z + later)

    load_u.wait()
    for q in range(FEAT // 128):
        u_all[x, :, q * 128 : (q + 1) * 128] = up_v[pl.ds(q, AD * RANK, stride=4), :].astype(BF16)
    arrived(d_all, 0, "right").wait_recv()
    share(d_all, 0, "far_right").start()
    arrived(d_all, 0, "left").wait_recv()
    share(d_all, 0, "far_left").start()
    share(u_all, 4, "right").start()
    share(u_all, 4, "left").start()

    def ring_step(direction, step, half):
        ring(direction, step - 1, half).wait_recv()
        source, landing, _ = ((sp, rp, 1), (sm, rm, -1))[direction]
        rows = half_rows[half]
        own = part[2 * step - 1 + direction, rows]
        source[step, rows] = (landing[step - 1, rows].astype(F32) + own).astype(BF16)
        ring(direction, step, half).start()

    lane = lax.broadcasted_iota(I32, (BLK // 2, 128), 1)
    eye = lax.broadcasted_iota(I32, (BLK, 128), 0) == lax.broadcasted_iota(I32, (BLK, 128), 1)
    lane_adapter = (lax.broadcasted_iota(I32, (BLK, SLAB_W), 1) // RANK + 1).astype(F32)

    def adapter_mask(q):
        wanted = jnp.sum(jnp.where(eye, ids_r[q], 0.0), axis=1, keepdims=True)
        return lane_adapter == wanted

    def to_reducer(q):
        return pltpu.make_async_remote_copy(
            src_ref=low_s.at[q],
            dst_ref=red.at[flat],
            send_sem=low_send.at[q],
            recv_sem=red_recv.at[flat],
            device_id=(g, q // 2, q % 2),
            device_id_type=MESH,
        )

    def from_device(i):
        return pltpu.make_async_remote_copy(
            src_ref=red.at[i],
            dst_ref=red.at[i],
            send_sem=low_send.at[0],
            recv_sem=red_recv.at[i],
            device_id=(g, (r + 1) % NROW, c),
            device_id_type=MESH,
        )

    def to_all(q, i):
        return pltpu.make_async_remote_copy(
            src_ref=low_full.at[q],
            dst_ref=low_full.at[q],
            send_sem=full_send.at[i],
            recv_sem=full_recv.at[q],
            device_id=(g, (r + i // 2) % NROW, (c + i % 2) % 2),
            device_id_type=MESH,
        )

    def project(chunk):
        first, last = chunk
        for q in range(first, last):

            @pl.when(z != q)
            def _():
                take_ids(q).wait_recv()
                take_rows(q).wait_recv()

        projected = lax.dot_general(
            xr[first:last].reshape((last - first) * BLK, FEAT),
            d_all[...].reshape(SLAB_W, FEAT),
            (((1,), (1,)), ((), ())),
            preferred_element_type=F32,
        )
        for q in range(first, last):
            block = projected[(q - first) * BLK : (q - first + 1) * BLK]
            block = jnp.where(adapter_mask(q), block, 0.0)
            folded = block[:, 0:128]
            for k in range(1, SLAB_W // 128):
                folded += block[:, k * 128 : (k + 1) * 128]
            folded += pltpu.roll(folded, RANK, 1)
            low_s[q] = jnp.where(lane < RANK, folded[: BLK // 2], folded[BLK // 2 :])

            @pl.when(flat != q)
            def _():
                to_reducer(q).start()

            @pl.when(flat == q)
            def _():
                red[flat] = low_s[q]

    def reduce_low(chunk):
        for q in range(*chunk):

            @pl.when(flat == q)
            def _():
                for i in range(NFLAT):
                    if i != q:
                        from_device(i).wait_recv()
                total = red[0]
                for i in range(1, NFLAT):
                    total += red[i]
                low_full[q] = total

                def hand_out(i, carry):
                    to_all(q, i).start()
                    return carry

                lax.fori_loop(1, NFLAT, hand_out, 0)

    def expand(chunk):
        first, last = chunk
        spread = []
        for q in range(first, last):

            @pl.when(flat != q)
            def _():
                to_all(q, 1).wait_recv()

            packed = low_full[q]
            turned = pltpu.roll(packed, RANK, 1)
            both = jnp.concatenate(
                [jnp.where(lane < RANK, packed, turned), jnp.where(lane < RANK, turned, packed)],
                axis=0,
            )
            wide = jnp.concatenate([both] * (SLAB_W // 128), axis=1)
            spread.append(jnp.where(adapter_mask(q), wide, 0.0).astype(BF16))
        delta = jnp.dot(
            jnp.concatenate(spread, axis=0),
            u_all[...].reshape(SLAB_W, FEAT),
            preferred_element_type=F32,
        ).astype(BF16)
        back_s[first:last] = delta.reshape(last - first, BLK, FEAT)
        for q in range(first, last):

            @pl.when(z != q)
            def _():
                send_back(q).start()

            @pl.when(z == q)
            def _():
                back_r[q] = back_s[q]

    ring_step(0, 1, 0)
    ring_step(1, 1, 1)
    arrived(d_all, 0, "far_right").wait_recv()
    arrived(d_all, 0, "far_left").wait_recv()
    project(CHUNKS[0])
    ring_step(0, 2, 1)
    ring_step(1, 2, 0)
    ring_step(0, 2, 0)
    ring_step(1, 2, 1)
    reduce_low(CHUNKS[0])
    arrived(u_all, 4, "right").wait_recv()
    share(u_all, 4, "far_right").start()
    arrived(u_all, 4, "left").wait_recv()
    share(u_all, 4, "far_left").start()
    project(CHUNKS[1])
    arrived(u_all, 4, "far_right").wait_recv()
    arrived(u_all, 4, "far_left").wait_recv()
    expand(CHUNKS[0])
    ring_step(0, 3, 1)
    ring_step(1, 3, 0)
    ring_step(0, 3, 0)
    ring_step(1, 3, 1)
    reduce_low(CHUNKS[1])
    expand(CHUNKS[1])
    project(CHUNKS[2])
    reduce_low(CHUNKS[2])
    expand(CHUNKS[2])

    for half in (1, 0):
        ring(0, 3, half).wait_recv()
        ring(1, 3, 1 - half).wait_recv()
    acc[...] = part[7] + (rp[3].astype(F32) + rm[3].astype(F32))

    for q in range(NZ):

        @pl.when(z != q)
        def _():
            take_back(q).wait_recv()

    added = lax.dot_general(
        choose[...],
        back_r[...].reshape(NZ * BLK, FEAT),
        (((0,), (0,)), ((), ())),
        preferred_element_type=F32,
    )
    out_ref[...] = (acc[...] + added).astype(BF16)

    swap_a.wait_send()
    for q in range(NZ):

        @pl.when(z != q)
        def _():
            send_ids(q).wait_send()
            send_rows(q).wait_send()
            send_back(q).wait_send()

    for buffer, base in ((d_all, 0), (u_all, 4)):
        for kind in ("right", "left", "far_right", "far_left"):
            share(buffer, base, kind).wait_send()
    for direction in (0, 1):
        ring(direction, 0, direction).wait_send()
        for step in (1, 2, 3):
            for half in (0, 1):
                ring(direction, step, half).wait_send()
    for q in range(NZ):

        @pl.when(flat != q)
        def _():
            to_reducer(q).wait_send()

        @pl.when(flat == q)
        def _():
            def left(i, carry):
                to_all(q, i).wait_send()
                return carry

            lax.fori_loop(1, NFLAT, left, 0)


def per_device(
    activations,
    base_weight_codes,
    block_scale_exponents,
    adapter_down_weight,
    adapter_up_weight,
    row_adapter_index,
    adapter_storage_slot,
):
    down = jnp.transpose(adapter_down_weight, (0, 2, 1)).reshape(AD * RANK, FEAT)
    up = adapter_up_weight.reshape(AD * RANK * FEAT // 128, 128)
    hbm = pl.BlockSpec(memory_space=pl.ANY)
    vmem = pl.BlockSpec(memory_space=pltpu.VMEM)
    dma = pltpu.SemaphoreType.DMA
    padded = NZ * BLK
    out = pl.pallas_call(
        kernel,
        out_shape=jax.ShapeDtypeStruct((ROWS, FEAT), BF16),
        in_specs=[hbm] * 5 + [vmem] * 2,
        out_specs=vmem,
        scratch_shapes=[
            pltpu.VMEM((2, ROWS, FEAT), BF16),
            pltpu.VMEM((NROW, 2 * FEAT, FEAT), BF16),
            pltpu.VMEM((32, NROW * FEAT), I32),
            pltpu.VMEM((AD * RANK, FEAT), F32),
            pltpu.VMEM((AD * RANK * FEAT // 128, 128), F32),
            pltpu.VMEM((1, 256), F32),
            pltpu.VMEM((padded, ROWS), BF16),
            pltpu.VMEM((NZ, BLK, FEAT), BF16),
            pltpu.VMEM((NZ, BLK, FEAT), BF16),
            pltpu.VMEM((NZ, 1, 128), F32),
            pltpu.VMEM((NZ, 1, 128), F32),
            pltpu.VMEM((NX, AD * RANK, FEAT), BF16),
            pltpu.VMEM((NX, AD * RANK, FEAT), BF16),
            pltpu.VMEM((NROW, ROWS, FEAT), F32),
            pltpu.VMEM((4, ROWS, FEAT), BF16),
            pltpu.VMEM((4, ROWS, FEAT), BF16),
            pltpu.VMEM((4, ROWS, FEAT), BF16),
            pltpu.VMEM((4, ROWS, FEAT), BF16),
            pltpu.VMEM((NZ, BLK // 2, 128), F32),
            pltpu.VMEM((NFLAT, BLK // 2, 128), F32),
            pltpu.VMEM((NZ, BLK // 2, 128), F32),
            pltpu.VMEM((NZ, BLK, FEAT), BF16),
            pltpu.VMEM((NZ, BLK, FEAT), BF16),
            pltpu.VMEM((ROWS, FEAT), F32),
            dma((4,)),
            dma((NROW,)),
            dma((2,)),
            dma((NZ,)),
            dma((NZ,)),
            dma((NZ,)),
            dma((NZ,)),
            dma((8,)),
            dma((8,)),
            dma((2, 4, 2)),
            dma((2, 4, 2)),
            dma((NZ,)),
            dma((NFLAT,)),
            dma((NFLAT,)),
            dma((NZ,)),
            dma((NZ,)),
            dma((NZ,)),
            pltpu.SemaphoreType.REGULAR((NZ,)),
        ],
        compiler_params=pltpu.CompilerParams(
            collective_id=0, has_side_effects=True, vmem_limit_bytes=56 * 1024 * 1024
        ),
        cost_estimate=pl.CostEstimate(
            flops=2 * ROWS * 2 * FEAT * NROW * FEAT, bytes_accessed=11 << 20, transcendentals=0
        ),
        name="projection",
    )(
        activations,
        base_weight_codes,
        block_scale_exponents,
        down,
        up,
        row_adapter_index.reshape(1, ROWS),
        adapter_storage_slot.reshape(1, -1),
    )
    return out.reshape(ROWS, 1, 1, FEAT)


def solution(mesh):
    return jax.shard_map(
        per_device,
        mesh=mesh,
        in_specs=(
            P("group", ("row", "col")),
            P("row", "col"),
            P("row", "col"),
            P("group", ("row", "col"), None),
            P("group", None, "col", "row", None),
            P("group"),
            P(),
        ),
        out_specs=P("group", "col", "row", None),
        check_vma=False,
    )
```

```python
import functools

import jax
import jax.numpy as jnp
from jax import lax
from jax.experimental import pallas as pl
from jax.experimental.pallas import tpu as pltpu
from jax.sharding import PartitionSpec as P

MESH = pl.DeviceIdType.MESH
F32 = jnp.float32
BF16 = jnp.bfloat16
I32 = jnp.int32

NX = 4
NZ = 12
NROW = 8
NFLAT = 16
ROWS = 256
FEAT = 512
BLK = 48
RANK = 64
AD = 4
SLAB_W = NX * AD * RANK

CHUNKS = ((0, 6), (6, 12))


def kernel(
    act_h,
    codes_h,
    scl_h,
    down_h,
    up_h,
    ids_ref,
    tab_ref,
    out_ref,
    a_all,
    w_v,
    scl_v,
    down_v,
    up_v,
    tab_v,
    choose,
    xs,
    xr,
    ids_s,
    ids_r,
    d_all,
    u_all,
    part,
    sp,
    sm,
    rp,
    rm,
    low_s,
    red,
    low_full,
    back_s,
    back_r,
    acc,
    load_sem,
    w_sem,
    a_sem,
    x_send,
    x_recv,
    i_send,
    i_recv,
    ad_send,
    ad_recv,
    rs_send,
    rs_recv,
    low_send,
    red_recv,
    full_send,
    full_recv,
    b_send,
    b_recv,
    hello,
):
    g = lax.axis_index("group")
    r = lax.axis_index("row")
    c = lax.axis_index("col")
    x = g // NZ
    z = g % NZ
    flat = 2 * r + c

    def at_z(there):
        return (x * NZ + there, r, c)

    def at_x(offset):
        return (((x + offset + NX) % NX) * NZ + z, r, c)

    def at_row(offset):
        return (g, (r + offset + NROW) % NROW, c)

    def block_of(i):
        return (r + 4 + ((i + 1) // 2) * (1 - 2 * (i % 2)) + NROW) % NROW

    load_a = pltpu.make_async_copy(act_h, a_all.at[c], load_sem.at[0])
    load_s = pltpu.make_async_copy(scl_h, scl_v, load_sem.at[1])
    load_d = pltpu.make_async_copy(down_h, down_v, load_sem.at[2])
    load_u = pltpu.make_async_copy(up_h, up_v, load_sem.at[3])

    def load_w(i):
        columns = pl.ds(pl.multiple_of(block_of(i) * FEAT, FEAT), FEAT)
        return pltpu.make_async_copy(codes_h.at[:, columns], w_v.at[i], w_sem.at[i])

    load_a.start()
    load_w(0).start()
    load_s.start()
    load_d.start()
    for i in range(1, NROW):
        load_w(i).start()
    load_u.start()

    barrier = pltpu.get_barrier_semaphore()
    for o in range(1, NX):
        pl.semaphore_signal(barrier, inc=1, device_id=at_x(o), device_id_type=MESH)

    def greet_later(there, carry):
        pl.semaphore_signal(barrier, inc=1, device_id=at_z(there), device_id_type=MESH)
        return carry

    def greet(i, carry):
        pl.semaphore_signal(
            barrier,
            inc=1,
            device_id=(g, (r + i // 2) % NROW, (c + i % 2) % 2),
            device_id_type=MESH,
        )
        return carry

    lax.fori_loop(1, NFLAT, greet, 0)
    lax.fori_loop(z + 1, NZ, greet_later, 0)

    pl.semaphore_wait(barrier, NX - 1 + NFLAT - 1 + z)

    def greet_earlier(there, carry):
        pl.semaphore_signal(hello.at[z], inc=1, device_id=at_z(there), device_id_type=MESH)
        return carry

    lax.fori_loop(0, z, greet_earlier, 0)

    tab_v[...] = jnp.zeros(tab_v.shape, F32)
    tab_v[:, : tab_ref.shape[1]] = tab_ref[...].astype(F32)
    ids = ids_ref[...]
    match = (lax.broadcasted_iota(I32, (256, ROWS), 0) == ids).astype(F32).astype(BF16)
    slots = jnp.dot(
        jnp.broadcast_to(tab_v[...], (8, 256)).astype(BF16), match, preferred_element_type=F32
    ).astype(I32)
    owner = slots >> 2
    owner_x = (
        (owner >= NZ).astype(I32) + (owner >= 2 * NZ).astype(I32) + (owner >= 3 * NZ).astype(I32)
    )
    place = owner - NZ * owner_x
    adapter = (owner_x * AD + (slots & 3) + 1).astype(F32).astype(BF16)
    sent_to = lax.broadcasted_iota(I32, (16, ROWS), 0) == place[0:1]
    before = (
        lax.broadcasted_iota(I32, (ROWS, ROWS), 0) < lax.broadcasted_iota(I32, (ROWS, ROWS), 1)
    )
    prefix = jnp.dot(
        sent_to.astype(F32).astype(BF16),
        before.astype(F32).astype(BF16),
        preferred_element_type=F32,
    )
    position = jnp.sum(jnp.where(sent_to, prefix, 0.0), axis=0, keepdims=True).astype(I32)
    target = place[0:1] * BLK + position

    swap_a = pltpu.make_async_remote_copy(
        src_ref=a_all.at[c],
        dst_ref=a_all.at[c],
        send_sem=a_sem.at[0],
        recv_sem=a_sem.at[1],
        device_id=(g, r, 1 - c),
        device_id_type=MESH,
    )
    take_a = pltpu.make_async_remote_copy(
        src_ref=a_all.at[1 - c],
        dst_ref=a_all.at[1 - c],
        send_sem=a_sem.at[0],
        recv_sem=a_sem.at[1],
        device_id=(g, r, 1 - c),
        device_id_type=MESH,
    )

    def share(buffer, base, kind):
        half = AD * RANK // 2
        where = {
            "right": (x, pl.ds(0, 2 * half), 1),
            "left": (x, pl.ds(0, 2 * half), -1),
            "far_right": ((x + NX - 1) % NX, pl.ds(0, half), 1),
            "far_left": ((x + 1) % NX, pl.ds(half, half), -1),
        }
        at, rows, step = where[kind]
        n = base + ("right", "left", "far_right", "far_left").index(kind)
        return pltpu.make_async_remote_copy(
            src_ref=buffer.at[at, rows],
            dst_ref=buffer.at[at, rows],
            send_sem=ad_send.at[n],
            recv_sem=ad_recv.at[n],
            device_id=at_x(step),
            device_id_type=MESH,
        )

    def arrived(buffer, base, kind):
        half = AD * RANK // 2
        where = {
            "right": ((x + NX - 1) % NX, pl.ds(0, 2 * half)),
            "left": ((x + 1) % NX, pl.ds(0, 2 * half)),
            "far_right": ((x + 2) % NX, pl.ds(0, half)),
            "far_left": ((x + 2) % NX, pl.ds(half, half)),
        }
        at, rows = where[kind]
        n = base + ("right", "left", "far_right", "far_left").index(kind)
        return pltpu.make_async_remote_copy(
            src_ref=buffer.at[at, rows],
            dst_ref=buffer.at[at, rows],
            send_sem=ad_send.at[n],
            recv_sem=ad_recv.at[n],
            device_id=at_x(1),
            device_id_type=MESH,
        )
    load_d.wait()
    d_all[x] = down_v[...].astype(BF16)
    share(d_all, 0, "right").start()
    share(d_all, 0, "left").start()
    load_a.wait()
    swap_a.start()

    choose[...] = (
        (lax.broadcasted_iota(I32, (NZ * BLK, ROWS), 0) == target).astype(F32).astype(BF16)
    )
    ids_s[...] = jnp.zeros(ids_s.shape, F32)
    for q in range(NZ):
        row = lax.dot_general(
            adapter,
            choose[q * BLK : (q + 1) * BLK, :],
            (((1,), (1,)), ((), ())),
            preferred_element_type=F32,
        )
        ids_s[q, :, 0:BLK] = row[0:1]
    ids_r[z] = ids_s[z]
    xs[...] = (
        jnp.dot(choose[...], a_all[c], preferred_element_type=F32)
        .astype(BF16)
        .reshape(NZ, BLK, FEAT)
    )
    xr[z] = xs[z]

    def send_rows(there):
        return pltpu.make_async_remote_copy(
            src_ref=xs.at[there],
            dst_ref=xr.at[z],
            send_sem=x_send.at[there],
            recv_sem=x_recv.at[z],
            device_id=at_z(there),
            device_id_type=MESH,
        )

    def take_rows(there):
        return pltpu.make_async_remote_copy(
            src_ref=xr.at[there],
            dst_ref=xr.at[there],
            send_sem=x_send.at[there],
            recv_sem=x_recv.at[there],
            device_id=at_z(there),
            device_id_type=MESH,
        )

    def send_ids(there):
        return pltpu.make_async_remote_copy(
            src_ref=ids_s.at[there],
            dst_ref=ids_r.at[z],
            send_sem=i_send.at[there],
            recv_sem=i_recv.at[z],
            device_id=at_z(there),
            device_id_type=MESH,
        )

    def take_ids(there):
        return pltpu.make_async_remote_copy(
            src_ref=ids_r.at[there],
            dst_ref=ids_r.at[there],
            send_sem=i_send.at[there],
            recv_sem=i_recv.at[there],
            device_id=at_z(there),
            device_id_type=MESH,
        )

    def send_back(there):
        return pltpu.make_async_remote_copy(
            src_ref=back_s.at[there],
            dst_ref=back_r.at[z],
            send_sem=b_send.at[there],
            recv_sem=b_recv.at[z],
            device_id=at_z(there),
            device_id_type=MESH,
        )

    def take_back(there):
        return pltpu.make_async_remote_copy(
            src_ref=back_r.at[there],
            dst_ref=back_r.at[there],
            send_sem=b_send.at[there],
            recv_sem=b_recv.at[there],
            device_id=at_z(there),
            device_id_type=MESH,
        )

    def post_earlier(k, carry):
        there = jnp.where(k % 2 == 0, k // 2, z - 1 - k // 2)
        send_ids(there).start()
        send_rows(there).start()
        return carry

    lax.fori_loop(0, z, post_earlier, 0)

    def post_later(there):
        @pl.when(there < NZ)
        def _():
            pl.semaphore_wait(hello.at[there], 1)
            send_ids(there).start()
            send_rows(there).start()

    half_rows = (pl.ds(0, ROWS // 2), pl.ds(ROWS // 2, ROWS // 2))

    def ring(direction, step, half):
        source, landing, way = ((sp, rp, 1), (sm, rm, -1))[direction]
        return pltpu.make_async_remote_copy(
            src_ref=source.at[step, half_rows[half]],
            dst_ref=landing.at[step, half_rows[half]],
            send_sem=rs_send.at[direction, step, half],
            recv_sem=rs_recv.at[direction, step, half],
            device_id=at_row(way),
            device_id_type=MESH,
        )

    load_s.wait()
    take_a.wait_recv()

    def base_block(i, carry):
        load_w(i).wait()
        columns = pl.ds(pl.multiple_of(block_of(i) * FEAT, FEAT), FEAT)
        scale = jnp.exp2(scl_v[:, columns].astype(F32)).astype(BF16)
        weight = (w_v[i].reshape(32, 32, FEAT) * scale[:, None, :]).reshape(2 * FEAT, FEAT)
        value = jnp.dot(a_all[0], weight[:FEAT], preferred_element_type=F32)
        value += jnp.dot(a_all[1], weight[FEAT:], preferred_element_type=F32)
        part[i] = value

        @pl.when(i == 0)
        def _():
            sp[0, half_rows[0]] = part[0, half_rows[0]].astype(BF16)
            ring(0, 0, 0).start()
            sm[0, half_rows[1]] = part[0, half_rows[1]].astype(BF16)
            ring(1, 0, 1).start()

        @pl.when(i == 1)
        def _():
            sp[1, half_rows[1]] = part[1, half_rows[1]].astype(BF16)
            ring(0, 1, 1).start()

        @pl.when(i == 2)
        def _():
            sm[1, half_rows[0]] = part[2, half_rows[0]].astype(BF16)
            ring(1, 1, 0).start()

        post_later(z + 1 + i)
        return carry

    lax.fori_loop(0, NROW, base_block, 0)
    for later in range(NROW + 1, NZ):
        post_later(z + later)

    load_u.wait()
    for q in range(FEAT // 128):
        u_all[x, :, q * 128 : (q + 1) * 128] = up_v[pl.ds(q, AD * RANK, stride=4), :].astype(BF16)
    arrived(d_all, 0, "right").wait_recv()
    share(d_all, 0, "far_right").start()
    arrived(d_all, 0, "left").wait_recv()
    share(d_all, 0, "far_left").start()
    share(u_all, 4, "right").start()
    share(u_all, 4, "left").start()

    def ring_step(direction, step, half):
        ring(direction, step - 1, half).wait_recv()
        source, landing, _ = ((sp, rp, 1), (sm, rm, -1))[direction]
        rows = half_rows[half]
        own = part[2 * step - 1 + direction, rows]
        source[step, rows] = (landing[step - 1, rows].astype(F32) + own).astype(BF16)
        ring(direction, step, half).start()

    lane = lax.broadcasted_iota(I32, (BLK // 2, 128), 1)
    eye = lax.broadcasted_iota(I32, (BLK, 128), 0) == lax.broadcasted_iota(I32, (BLK, 128), 1)
    lane_adapter = (lax.broadcasted_iota(I32, (BLK, SLAB_W), 1) // RANK + 1).astype(F32)

    def adapter_mask(q):
        wanted = jnp.sum(jnp.where(eye, ids_r[q], 0.0), axis=1, keepdims=True)
        return lane_adapter == wanted

    def reducer(p):
        return (3 * p) % NROW, p % 2

    def adds_up(p):
        row, col = reducer(p)
        return flat == 2 * row + col

    def to_reducer(p):
        row, col = reducer(p)
        return pltpu.make_async_remote_copy(
            src_ref=low_s.at[p],
            dst_ref=red.at[flat],
            send_sem=low_send.at[p],
            recv_sem=red_recv.at[flat],
            device_id=(g, row, col),
            device_id_type=MESH,
        )

    def from_device(i):
        return pltpu.make_async_remote_copy(
            src_ref=red.at[i],
            dst_ref=red.at[i],
            send_sem=low_send.at[0],
            recv_sem=red_recv.at[i],
            device_id=(g, (r + 1) % NROW, c),
            device_id_type=MESH,
        )

    def to_all(p, i):
        return pltpu.make_async_remote_copy(
            src_ref=low_full.at[p],
            dst_ref=low_full.at[p],
            send_sem=full_send.at[i],
            recv_sem=full_recv.at[p],
            device_id=(g, (r + i // 2) % NROW, (c + i % 2) % 2),
            device_id_type=MESH,
        )

    def project(chunk):
        first, last = chunk
        for q in range(first, last):

            @pl.when(z != q)
            def _():
                take_ids(q).wait_recv()
                take_rows(q).wait_recv()

        projected = lax.dot_general(
            xr[first:last].reshape((last - first) * BLK, FEAT),
            d_all[...].reshape(SLAB_W, FEAT),
            (((1,), (1,)), ((), ())),
            preferred_element_type=F32,
        )
        for p in range(first // 2, last // 2):
            halves = []
            for q in (2 * p, 2 * p + 1):
                block = projected[(q - first) * BLK : (q - first + 1) * BLK]
                block = jnp.where(adapter_mask(q), block, 0.0)
                folded = block[:, 0:128]
                for k in range(1, SLAB_W // 128):
                    folded += block[:, k * 128 : (k + 1) * 128]
                folded += pltpu.roll(folded, RANK, 1)
                halves.append(jnp.where(lane < RANK, folded[: BLK // 2], folded[BLK // 2 :]))
            low_s[p] = jnp.concatenate(halves, axis=0).astype(BF16)

            @pl.when(jnp.logical_not(adds_up(p)))
            def _():
                to_reducer(p).start()

            @pl.when(adds_up(p))
            def _():
                red[flat] = low_s[p]

    def reduce_low(chunk):
        for p in range(chunk[0] // 2, chunk[1] // 2):

            @pl.when(adds_up(p))
            def _():
                row, col = reducer(p)
                for i in range(NFLAT):
                    if i != 2 * row + col:
                        from_device(i).wait_recv()
                total = red[0].astype(F32)
                for i in range(1, NFLAT):
                    total += red[i].astype(F32)
                low_full[p] = total.astype(BF16)

                def hand_out(i, carry):
                    to_all(p, i).start()
                    return carry

                lax.fori_loop(1, NFLAT, hand_out, 0)

    def expand(chunk):
        first, last = chunk
        spread = []
        for p in range(first // 2, last // 2):

            @pl.when(jnp.logical_not(adds_up(p)))
            def _():
                to_all(p, 1).wait_recv()

            summed = low_full[p].astype(F32)
            for q in (2 * p, 2 * p + 1):
                packed = summed[(q % 2) * (BLK // 2) : (q % 2 + 1) * (BLK // 2)]
                turned = pltpu.roll(packed, RANK, 1)
                both = jnp.concatenate(
                    [
                        jnp.where(lane < RANK, packed, turned),
                        jnp.where(lane < RANK, turned, packed),
                    ],
                    axis=0,
                )
                wide = jnp.concatenate([both] * (SLAB_W // 128), axis=1)
                spread.append(jnp.where(adapter_mask(q), wide, 0.0).astype(BF16))
        delta = jnp.dot(
            jnp.concatenate(spread, axis=0),
            u_all[...].reshape(SLAB_W, FEAT),
            preferred_element_type=F32,
        ).astype(BF16)
        back_s[first:last] = delta.reshape(last - first, BLK, FEAT)
        for q in range(first, last):

            @pl.when(z != q)
            def _():
                send_back(q).start()

            @pl.when(z == q)
            def _():
                back_r[q] = back_s[q]

    ring_step(0, 1, 0)
    ring_step(1, 1, 1)
    arrived(d_all, 0, "far_right").wait_recv()
    arrived(d_all, 0, "far_left").wait_recv()
    project(CHUNKS[0])
    ring_step(0, 2, 1)
    ring_step(1, 2, 0)
    ring_step(0, 2, 0)
    ring_step(1, 2, 1)
    reduce_low(CHUNKS[0])
    arrived(u_all, 4, "right").wait_recv()
    share(u_all, 4, "far_right").start()
    arrived(u_all, 4, "left").wait_recv()
    share(u_all, 4, "far_left").start()
    project(CHUNKS[1])
    arrived(u_all, 4, "far_right").wait_recv()
    arrived(u_all, 4, "far_left").wait_recv()
    expand(CHUNKS[0])
    reduce_low(CHUNKS[1])
    ring_step(0, 3, 1)
    ring_step(1, 3, 0)
    ring_step(0, 3, 0)
    ring_step(1, 3, 1)
    expand(CHUNKS[1])

    for half in (1, 0):
        ring(0, 3, half).wait_recv()
        ring(1, 3, 1 - half).wait_recv()
    acc[...] = part[7] + (rp[3].astype(F32) + rm[3].astype(F32))

    for q in range(NZ):

        @pl.when(z != q)
        def _():
            take_back(q).wait_recv()

    added = lax.dot_general(
        choose[...],
        back_r[...].reshape(NZ * BLK, FEAT),
        (((0,), (0,)), ((), ())),
        preferred_element_type=F32,
    )
    out_ref[...] = (acc[...] + added).astype(BF16)

    swap_a.wait_send()
    for q in range(NZ):

        @pl.when(z != q)
        def _():
            send_ids(q).wait_send()
            send_rows(q).wait_send()
            send_back(q).wait_send()

    for buffer, base in ((d_all, 0), (u_all, 4)):
        for kind in ("right", "left", "far_right", "far_left"):
            share(buffer, base, kind).wait_send()
    for direction in (0, 1):
        ring(direction, 0, direction).wait_send()
        for step in (1, 2, 3):
            for half in (0, 1):
                ring(direction, step, half).wait_send()
    for p in range(NZ // 2):

        @pl.when(jnp.logical_not(adds_up(p)))
        def _():
            to_reducer(p).wait_send()

        @pl.when(adds_up(p))
        def _():
            def left(i, carry):
                to_all(p, i).wait_send()
                return carry

            lax.fori_loop(1, NFLAT, left, 0)


def per_device(
    activations,
    base_weight_codes,
    block_scale_exponents,
    adapter_down_weight,
    adapter_up_weight,
    row_adapter_index,
    adapter_storage_slot,
):
    down = jnp.transpose(adapter_down_weight, (0, 2, 1)).reshape(AD * RANK, FEAT)
    up = adapter_up_weight.reshape(AD * RANK * FEAT // 128, 128)
    hbm = pl.BlockSpec(memory_space=pl.ANY)
    vmem = pl.BlockSpec(memory_space=pltpu.VMEM)
    dma = pltpu.SemaphoreType.DMA
    padded = NZ * BLK
    out = pl.pallas_call(
        kernel,
        out_shape=jax.ShapeDtypeStruct((ROWS, FEAT), BF16),
        in_specs=[hbm] * 5 + [vmem] * 2,
        out_specs=vmem,
        scratch_shapes=[
            pltpu.VMEM((2, ROWS, FEAT), BF16),
            pltpu.VMEM((NROW, 2 * FEAT, FEAT), BF16),
            pltpu.VMEM((32, NROW * FEAT), I32),
            pltpu.VMEM((AD * RANK, FEAT), F32),
            pltpu.VMEM((AD * RANK * FEAT // 128, 128), F32),
            pltpu.VMEM((1, 256), F32),
            pltpu.VMEM((padded, ROWS), BF16),
            pltpu.VMEM((NZ, BLK, FEAT), BF16),
            pltpu.VMEM((NZ, BLK, FEAT), BF16),
            pltpu.VMEM((NZ, 1, 128), F32),
            pltpu.VMEM((NZ, 1, 128), F32),
            pltpu.VMEM((NX, AD * RANK, FEAT), BF16),
            pltpu.VMEM((NX, AD * RANK, FEAT), BF16),
            pltpu.VMEM((NROW, ROWS, FEAT), F32),
            pltpu.VMEM((4, ROWS, FEAT), BF16),
            pltpu.VMEM((4, ROWS, FEAT), BF16),
            pltpu.VMEM((4, ROWS, FEAT), BF16),
            pltpu.VMEM((4, ROWS, FEAT), BF16),
            pltpu.VMEM((NZ // 2, BLK, 128), BF16),
            pltpu.VMEM((NFLAT, BLK, 128), BF16),
            pltpu.VMEM((NZ // 2, BLK, 128), BF16),
            pltpu.VMEM((NZ, BLK, FEAT), BF16),
            pltpu.VMEM((NZ, BLK, FEAT), BF16),
            pltpu.VMEM((ROWS, FEAT), F32),
            dma((4,)),
            dma((NROW,)),
            dma((2,)),
            dma((NZ,)),
            dma((NZ,)),
            dma((NZ,)),
            dma((NZ,)),
            dma((8,)),
            dma((8,)),
            dma((2, 4, 2)),
            dma((2, 4, 2)),
            dma((NZ // 2,)),
            dma((NFLAT,)),
            dma((NFLAT,)),
            dma((NZ // 2,)),
            dma((NZ,)),
            dma((NZ,)),
            pltpu.SemaphoreType.REGULAR((NZ,)),
        ],
        compiler_params=pltpu.CompilerParams(
            collective_id=0, has_side_effects=True, vmem_limit_bytes=56 * 1024 * 1024
        ),
        cost_estimate=pl.CostEstimate(
            flops=2 * ROWS * 2 * FEAT * NROW * FEAT, bytes_accessed=11 << 20, transcendentals=0
        ),
        name="projection",
    )(
        activations,
        base_weight_codes,
        block_scale_exponents,
        down,
        up,
        row_adapter_index.reshape(1, ROWS),
        adapter_storage_slot.reshape(1, -1),
    )
    return out.reshape(ROWS, 1, 1, FEAT)


def solution(mesh):
    return jax.shard_map(
        per_device,
        mesh=mesh,
        in_specs=(
            P("group", ("row", "col")),
            P("row", "col"),
            P("row", "col"),
            P("group", ("row", "col"), None),
            P("group", None, "col", "row", None),
            P("group"),
            P(),
        ),
        out_specs=P("group", "col", "row", None),
        check_vma=False,
    )
```

```python
import functools

import jax
import jax.numpy as jnp
from jax import lax
from jax.experimental import pallas as pl
from jax.experimental.pallas import tpu as pltpu
from jax.sharding import PartitionSpec as P

MESH = pl.DeviceIdType.MESH
F32 = jnp.float32
BF16 = jnp.bfloat16
I32 = jnp.int32

NX = 4
NZ = 12
NROW = 8
NFLAT = 16
ROWS = 256
FEAT = 512
BLK = 48
RANK = 64
AD = 4
SLAB_W = NX * AD * RANK

CHUNKS = ((0, 1), (2, 3), (4, 5))


def kernel(
    act_h,
    codes_h,
    scl_h,
    down_h,
    up_h,
    ids_ref,
    tab_ref,
    out_ref,
    a_all,
    w_v,
    scl_v,
    down_v,
    up_v,
    tab_v,
    choose,
    xs,
    xr,
    ids_s,
    ids_r,
    d_all,
    u_all,
    part,
    sp,
    sm,
    rp,
    rm,
    low_s,
    red,
    low_full,
    back_s,
    back_r,
    acc,
    load_sem,
    w_sem,
    a_sem,
    x_send,
    x_recv,
    i_send,
    i_recv,
    ad_send,
    ad_recv,
    rs_send,
    rs_recv,
    low_send,
    red_recv,
    full_send,
    full_recv,
    b_send,
    b_recv,
    hello,
):
    g = lax.axis_index("group")
    r = lax.axis_index("row")
    c = lax.axis_index("col")
    x = g // NZ
    z = g % NZ
    flat = 2 * r + c

    def at_z(there):
        return (x * NZ + there, r, c)

    def at_x(offset):
        return (((x + offset + NX) % NX) * NZ + z, r, c)

    def at_row(offset):
        return (g, (r + offset + NROW) % NROW, c)

    def block_of(i):
        return (r + 4 + ((i + 1) // 2) * (1 - 2 * (i % 2)) + NROW) % NROW

    load_a = pltpu.make_async_copy(act_h, a_all.at[c], load_sem.at[0])
    load_s = pltpu.make_async_copy(scl_h, scl_v, load_sem.at[1])
    load_d = pltpu.make_async_copy(down_h, down_v, load_sem.at[2])
    load_u = pltpu.make_async_copy(up_h, up_v, load_sem.at[3])

    def load_w(i):
        columns = pl.ds(pl.multiple_of(block_of(i) * FEAT, FEAT), FEAT)
        return pltpu.make_async_copy(codes_h.at[:, columns], w_v.at[i], w_sem.at[i])

    load_a.start()
    load_d.start()
    load_u.start()
    load_w(0).start()
    load_s.start()
    for i in range(1, NROW):
        load_w(i).start()

    barrier = pltpu.get_barrier_semaphore()
    for o in range(1, NX):
        pl.semaphore_signal(barrier, inc=1, device_id=at_x(o), device_id_type=MESH)

    def greet_later(there, carry):
        pl.semaphore_signal(barrier, inc=1, device_id=at_z(there), device_id_type=MESH)
        return carry

    def greet(i, carry):
        pl.semaphore_signal(
            barrier,
            inc=1,
            device_id=(g, (r + i // 2) % NROW, (c + i % 2) % 2),
            device_id_type=MESH,
        )
        return carry

    lax.fori_loop(1, NFLAT, greet, 0)
    lax.fori_loop(z + 1, NZ, greet_later, 0)

    pl.semaphore_wait(barrier, NX - 1 + NFLAT - 1 + z)

    def greet_earlier(there, carry):
        pl.semaphore_signal(hello.at[z], inc=1, device_id=at_z(there), device_id_type=MESH)
        return carry

    lax.fori_loop(0, z, greet_earlier, 0)

    tab_v[...] = jnp.zeros(tab_v.shape, F32)
    tab_v[:, : tab_ref.shape[1]] = tab_ref[...].astype(F32)
    ids = ids_ref[...]
    match = (lax.broadcasted_iota(I32, (256, ROWS), 0) == ids).astype(F32).astype(BF16)
    slots = jnp.dot(
        jnp.broadcast_to(tab_v[...], (8, 256)).astype(BF16), match, preferred_element_type=F32
    ).astype(I32)
    owner = slots >> 2
    owner_x = (
        (owner >= NZ).astype(I32) + (owner >= 2 * NZ).astype(I32) + (owner >= 3 * NZ).astype(I32)
    )
    place = owner - NZ * owner_x
    adapter = (owner_x * AD + (slots & 3) + 1).astype(F32).astype(BF16)
    sent_to = lax.broadcasted_iota(I32, (16, ROWS), 0) == place[0:1]
    before = (
        lax.broadcasted_iota(I32, (ROWS, ROWS), 0) < lax.broadcasted_iota(I32, (ROWS, ROWS), 1)
    )
    prefix = jnp.dot(
        sent_to.astype(F32).astype(BF16),
        before.astype(F32).astype(BF16),
        preferred_element_type=F32,
    )
    position = jnp.sum(jnp.where(sent_to, prefix, 0.0), axis=0, keepdims=True).astype(I32)
    target = place[0:1] * BLK + position

    swap_a = pltpu.make_async_remote_copy(
        src_ref=a_all.at[c],
        dst_ref=a_all.at[c],
        send_sem=a_sem.at[0],
        recv_sem=a_sem.at[1],
        device_id=(g, r, 1 - c),
        device_id_type=MESH,
    )
    take_a = pltpu.make_async_remote_copy(
        src_ref=a_all.at[1 - c],
        dst_ref=a_all.at[1 - c],
        send_sem=a_sem.at[0],
        recv_sem=a_sem.at[1],
        device_id=(g, r, 1 - c),
        device_id_type=MESH,
    )

    def share(buffer, base, step):
        return pltpu.make_async_remote_copy(
            src_ref=buffer.at[x],
            dst_ref=buffer.at[x],
            send_sem=ad_send.at[base + step],
            recv_sem=ad_recv.at[base + step],
            device_id=at_x(step),
            device_id_type=MESH,
        )

    def arrived(buffer, base, step):
        return pltpu.make_async_remote_copy(
            src_ref=buffer.at[(x + NX - step) % NX],
            dst_ref=buffer.at[(x + NX - step) % NX],
            send_sem=ad_send.at[base + step],
            recv_sem=ad_recv.at[base + step],
            device_id=at_x(step),
            device_id_type=MESH,
        )

    load_d.wait()
    d_all[x] = down_v[...].astype(BF16)
    for step in (2, 1, 3):
        share(d_all, 0, step).start()
    load_a.wait()
    swap_a.start()

    choose[...] = (
        (lax.broadcasted_iota(I32, (NZ * BLK, ROWS), 0) == target).astype(F32).astype(BF16)
    )
    ids_s[...] = jnp.zeros(ids_s.shape, F32)
    for q in range(NZ):
        row = lax.dot_general(
            adapter,
            choose[q * BLK : (q + 1) * BLK, :],
            (((1,), (1,)), ((), ())),
            preferred_element_type=F32,
        )
        ids_s[q, :, 0:BLK] = row[0:1]
    ids_r[z] = ids_s[z]
    xs[...] = (
        jnp.dot(choose[...], a_all[c], preferred_element_type=F32)
        .astype(BF16)
        .reshape(NZ, BLK, FEAT)
    )
    xr[z] = xs[z]

    def send_rows(there):
        return pltpu.make_async_remote_copy(
            src_ref=xs.at[there],
            dst_ref=xr.at[z],
            send_sem=x_send.at[there],
            recv_sem=x_recv.at[z],
            device_id=at_z(there),
            device_id_type=MESH,
        )

    def take_rows(there):
        return pltpu.make_async_remote_copy(
            src_ref=xr.at[there],
            dst_ref=xr.at[there],
            send_sem=x_send.at[there],
            recv_sem=x_recv.at[there],
            device_id=at_z(there),
            device_id_type=MESH,
        )

    def send_ids(there):
        return pltpu.make_async_remote_copy(
            src_ref=ids_s.at[there],
            dst_ref=ids_r.at[z],
            send_sem=i_send.at[there],
            recv_sem=i_recv.at[z],
            device_id=at_z(there),
            device_id_type=MESH,
        )

    def take_ids(there):
        return pltpu.make_async_remote_copy(
            src_ref=ids_r.at[there],
            dst_ref=ids_r.at[there],
            send_sem=i_send.at[there],
            recv_sem=i_recv.at[there],
            device_id=at_z(there),
            device_id_type=MESH,
        )

    def send_back(there):
        return pltpu.make_async_remote_copy(
            src_ref=back_s.at[there],
            dst_ref=back_r.at[z],
            send_sem=b_send.at[there],
            recv_sem=b_recv.at[z],
            device_id=at_z(there),
            device_id_type=MESH,
        )

    def take_back(there):
        return pltpu.make_async_remote_copy(
            src_ref=back_r.at[there],
            dst_ref=back_r.at[there],
            send_sem=b_send.at[there],
            recv_sem=b_recv.at[there],
            device_id=at_z(there),
            device_id_type=MESH,
        )

    def post_earlier(k, carry):
        there = jnp.where(k % 2 == 0, k // 2, z - 1 - k // 2)
        send_ids(there).start()
        send_rows(there).start()
        return carry

    lax.fori_loop(0, z, post_earlier, 0)

    def post_later(there):
        @pl.when(there < NZ)
        def _():
            pl.semaphore_wait(hello.at[there], 1)
            send_ids(there).start()
            send_rows(there).start()

    load_u.wait()
    for q in range(FEAT // 128):
        u_all[x, :, q * 128 : (q + 1) * 128] = up_v[pl.ds(q, AD * RANK, stride=4), :].astype(BF16)
    for step in (2, 1, 3):
        share(u_all, 4, step).start()

    half_rows = (pl.ds(0, ROWS // 2), pl.ds(ROWS // 2, ROWS // 2))

    def ring(direction, step, half):
        source, landing, way = ((sp, rp, 1), (sm, rm, -1))[direction]
        return pltpu.make_async_remote_copy(
            src_ref=source.at[step, half_rows[half]],
            dst_ref=landing.at[step, half_rows[half]],
            send_sem=rs_send.at[direction, step, half],
            recv_sem=rs_recv.at[direction, step, half],
            device_id=at_row(way),
            device_id_type=MESH,
        )

    load_s.wait()
    take_a.wait_recv()

    def base_block(i, carry):
        load_w(i).wait()
        columns = pl.ds(pl.multiple_of(block_of(i) * FEAT, FEAT), FEAT)
        scale = jnp.exp2(scl_v[:, columns].astype(F32)).astype(BF16)
        weight = (w_v[i].reshape(32, 32, FEAT) * scale[:, None, :]).reshape(2 * FEAT, FEAT)
        value = jnp.dot(a_all[0], weight[:FEAT], preferred_element_type=F32)
        value += jnp.dot(a_all[1], weight[FEAT:], preferred_element_type=F32)
        part[i] = value

        @pl.when(i == 0)
        def _():
            sp[0, half_rows[0]] = part[0, half_rows[0]].astype(BF16)
            ring(0, 0, 0).start()
            sm[0, half_rows[1]] = part[0, half_rows[1]].astype(BF16)
            ring(1, 0, 1).start()

        @pl.when(i == 1)
        def _():
            sp[1, half_rows[1]] = part[1, half_rows[1]].astype(BF16)
            ring(0, 1, 1).start()

        @pl.when(i == 2)
        def _():
            sm[1, half_rows[0]] = part[2, half_rows[0]].astype(BF16)
            ring(1, 1, 0).start()

        post_later(z + 1 + i)
        return carry

    lax.fori_loop(0, NROW, base_block, 0)
    for later in range(NROW + 1, NZ):
        post_later(z + later)

    def ring_step(direction, step, half):
        ring(direction, step - 1, half).wait_recv()
        source, landing, _ = ((sp, rp, 1), (sm, rm, -1))[direction]
        rows = half_rows[half]
        own = part[2 * step - 1 + direction, rows]
        source[step, rows] = (landing[step - 1, rows].astype(F32) + own).astype(BF16)
        ring(direction, step, half).start()

    lane = lax.broadcasted_iota(I32, (BLK // 2, 128), 1)
    eye = lax.broadcasted_iota(I32, (BLK, 128), 0) == lax.broadcasted_iota(I32, (BLK, 128), 1)
    lane_adapter = (lax.broadcasted_iota(I32, (BLK, SLAB_W), 1) // RANK + 1).astype(F32)

    def adapter_mask(q):
        wanted = jnp.sum(jnp.where(eye, ids_r[q], 0.0), axis=1, keepdims=True)
        return lane_adapter == wanted

    def reducer(p):
        return (3 * p) % NROW, p % 2

    def adds_up(p):
        row, col = reducer(p)
        return flat == 2 * row + col

    def to_reducer(p):
        row, col = reducer(p)
        return pltpu.make_async_remote_copy(
            src_ref=low_s.at[p],
            dst_ref=red.at[flat],
            send_sem=low_send.at[p],
            recv_sem=red_recv.at[flat],
            device_id=(g, row, col),
            device_id_type=MESH,
        )

    def from_device(i):
        return pltpu.make_async_remote_copy(
            src_ref=red.at[i],
            dst_ref=red.at[i],
            send_sem=low_send.at[0],
            recv_sem=red_recv.at[i],
            device_id=(g, (r + 1) % NROW, c),
            device_id_type=MESH,
        )

    def to_all(p, i):
        return pltpu.make_async_remote_copy(
            src_ref=low_full.at[p],
            dst_ref=low_full.at[p],
            send_sem=full_send.at[i],
            recv_sem=full_recv.at[p],
            device_id=(g, (r + i // 2) % NROW, (c + i % 2) % 2),
            device_id_type=MESH,
        )

    def sources(chunk):
        return [2 * p + k for p in chunk for k in (0, 1)]

    def project(chunk):
        for q in sources(chunk):

            @pl.when(z != q)
            def _():
                take_ids(q).wait_recv()
                take_rows(q).wait_recv()

        projected = lax.dot_general(
            jnp.concatenate([xr[q] for q in sources(chunk)], axis=0),
            d_all[...].reshape(SLAB_W, FEAT),
            (((1,), (1,)), ((), ())),
            preferred_element_type=F32,
        )
        for n, p in enumerate(chunk):
            halves = []
            for k, q in enumerate((2 * p, 2 * p + 1)):
                block = projected[(2 * n + k) * BLK : (2 * n + k + 1) * BLK]
                block = jnp.where(adapter_mask(q), block, 0.0)
                folded = block[:, 0:128]
                for m in range(1, SLAB_W // 128):
                    folded += block[:, m * 128 : (m + 1) * 128]
                folded += pltpu.roll(folded, RANK, 1)
                halves.append(jnp.where(lane < RANK, folded[: BLK // 2], folded[BLK // 2 :]))
            low_s[p] = jnp.concatenate(halves, axis=0).astype(BF16)

            @pl.when(jnp.logical_not(adds_up(p)))
            def _():
                to_reducer(p).start()

            @pl.when(adds_up(p))
            def _():
                red[flat] = low_s[p]

    def reduce_low(chunk):
        for p in chunk:

            @pl.when(adds_up(p))
            def _():
                row, col = reducer(p)
                for i in range(NFLAT):
                    if i != 2 * row + col:
                        from_device(i).wait_recv()
                total = red[0].astype(F32)
                for i in range(1, NFLAT):
                    total += red[i].astype(F32)
                low_full[p] = total.astype(BF16)

                def hand_out(i, carry):
                    to_all(p, i).start()
                    return carry

                lax.fori_loop(1, NFLAT, hand_out, 0)

    def expand(chunk):
        spread = []
        for p in chunk:

            @pl.when(jnp.logical_not(adds_up(p)))
            def _():
                to_all(p, 1).wait_recv()

            summed = low_full[p].astype(F32)
            for q in (2 * p, 2 * p + 1):
                packed = summed[(q % 2) * (BLK // 2) : (q % 2 + 1) * (BLK // 2)]
                turned = pltpu.roll(packed, RANK, 1)
                both = jnp.concatenate(
                    [
                        jnp.where(lane < RANK, packed, turned),
                        jnp.where(lane < RANK, turned, packed),
                    ],
                    axis=0,
                )
                wide = jnp.concatenate([both] * (SLAB_W // 128), axis=1)
                spread.append(jnp.where(adapter_mask(q), wide, 0.0).astype(BF16))
        delta = jnp.dot(
            jnp.concatenate(spread, axis=0),
            u_all[...].reshape(SLAB_W, FEAT),
            preferred_element_type=F32,
        ).astype(BF16)
        for n, q in enumerate(sources(chunk)):
            back_s[q] = delta[n * BLK : (n + 1) * BLK]

            @pl.when(z != q)
            def _():
                send_back(q).start()

            @pl.when(z == q)
            def _():
                back_r[q] = back_s[q]

    ring_step(0, 1, 0)
    ring_step(1, 1, 1)
    for step in range(1, NX):
        arrived(d_all, 0, step).wait_recv()
    project(CHUNKS[0])
    ring_step(0, 2, 1)
    ring_step(1, 2, 0)
    ring_step(0, 2, 0)
    ring_step(1, 2, 1)
    reduce_low(CHUNKS[0])
    project(CHUNKS[1])
    for step in range(1, NX):
        arrived(u_all, 4, step).wait_recv()
    expand(CHUNKS[0])
    reduce_low(CHUNKS[1])
    project(CHUNKS[2])
    expand(CHUNKS[1])
    reduce_low(CHUNKS[2])
    ring_step(0, 3, 1)
    ring_step(1, 3, 0)
    ring_step(0, 3, 0)
    ring_step(1, 3, 1)
    expand(CHUNKS[2])

    for half in (1, 0):
        ring(0, 3, half).wait_recv()
        ring(1, 3, 1 - half).wait_recv()
    acc[...] = part[7] + (rp[3].astype(F32) + rm[3].astype(F32))

    for q in range(NZ):

        @pl.when(z != q)
        def _():
            take_back(q).wait_recv()

    added = lax.dot_general(
        choose[...],
        back_r[...].reshape(NZ * BLK, FEAT),
        (((0,), (0,)), ((), ())),
        preferred_element_type=F32,
    )
    out_ref[...] = (acc[...] + added).astype(BF16)

    swap_a.wait_send()
    for q in range(NZ):

        @pl.when(z != q)
        def _():
            send_ids(q).wait_send()
            send_rows(q).wait_send()
            send_back(q).wait_send()

    for buffer, base in ((d_all, 0), (u_all, 4)):
        for step in range(1, NX):
            share(buffer, base, step).wait_send()
    for direction in (0, 1):
        ring(direction, 0, direction).wait_send()
        for step in (1, 2, 3):
            for half in (0, 1):
                ring(direction, step, half).wait_send()
    for p in range(NZ // 2):

        @pl.when(jnp.logical_not(adds_up(p)))
        def _():
            to_reducer(p).wait_send()

        @pl.when(adds_up(p))
        def _():
            def left(i, carry):
                to_all(p, i).wait_send()
                return carry

            lax.fori_loop(1, NFLAT, left, 0)


def per_device(
    activations,
    base_weight_codes,
    block_scale_exponents,
    adapter_down_weight,
    adapter_up_weight,
    row_adapter_index,
    adapter_storage_slot,
):
    down = jnp.transpose(adapter_down_weight, (0, 2, 1)).reshape(AD * RANK, FEAT)
    up = adapter_up_weight.reshape(AD * RANK * FEAT // 128, 128)
    hbm = pl.BlockSpec(memory_space=pl.ANY)
    vmem = pl.BlockSpec(memory_space=pltpu.VMEM)
    dma = pltpu.SemaphoreType.DMA
    padded = NZ * BLK
    out = pl.pallas_call(
        kernel,
        out_shape=jax.ShapeDtypeStruct((ROWS, FEAT), BF16),
        in_specs=[hbm] * 5 + [vmem] * 2,
        out_specs=vmem,
        scratch_shapes=[
            pltpu.VMEM((2, ROWS, FEAT), BF16),
            pltpu.VMEM((NROW, 2 * FEAT, FEAT), BF16),
            pltpu.VMEM((32, NROW * FEAT), I32),
            pltpu.VMEM((AD * RANK, FEAT), F32),
            pltpu.VMEM((AD * RANK * FEAT // 128, 128), F32),
            pltpu.VMEM((1, 256), F32),
            pltpu.VMEM((padded, ROWS), BF16),
            pltpu.VMEM((NZ, BLK, FEAT), BF16),
            pltpu.VMEM((NZ, BLK, FEAT), BF16),
            pltpu.VMEM((NZ, 1, 128), F32),
            pltpu.VMEM((NZ, 1, 128), F32),
            pltpu.VMEM((NX, AD * RANK, FEAT), BF16),
            pltpu.VMEM((NX, AD * RANK, FEAT), BF16),
            pltpu.VMEM((NROW, ROWS, FEAT), F32),
            pltpu.VMEM((4, ROWS, FEAT), BF16),
            pltpu.VMEM((4, ROWS, FEAT), BF16),
            pltpu.VMEM((4, ROWS, FEAT), BF16),
            pltpu.VMEM((4, ROWS, FEAT), BF16),
            pltpu.VMEM((NZ // 2, BLK, 128), BF16),
            pltpu.VMEM((NFLAT, BLK, 128), BF16),
            pltpu.VMEM((NZ // 2, BLK, 128), BF16),
            pltpu.VMEM((NZ, BLK, FEAT), BF16),
            pltpu.VMEM((NZ, BLK, FEAT), BF16),
            pltpu.VMEM((ROWS, FEAT), F32),
            dma((4,)),
            dma((NROW,)),
            dma((2,)),
            dma((NZ,)),
            dma((NZ,)),
            dma((NZ,)),
            dma((NZ,)),
            dma((8,)),
            dma((8,)),
            dma((2, 4, 2)),
            dma((2, 4, 2)),
            dma((NZ // 2,)),
            dma((NFLAT,)),
            dma((NFLAT,)),
            dma((NZ // 2,)),
            dma((NZ,)),
            dma((NZ,)),
            pltpu.SemaphoreType.REGULAR((NZ,)),
        ],
        compiler_params=pltpu.CompilerParams(
            collective_id=0, has_side_effects=True, vmem_limit_bytes=56 * 1024 * 1024
        ),
        cost_estimate=pl.CostEstimate(
            flops=2 * ROWS * 2 * FEAT * NROW * FEAT, bytes_accessed=11 << 20, transcendentals=0
        ),
        name="projection",
    )(
        activations,
        base_weight_codes,
        block_scale_exponents,
        down,
        up,
        row_adapter_index.reshape(1, ROWS),
        adapter_storage_slot.reshape(1, -1),
    )
    return out.reshape(ROWS, 1, 1, FEAT)


def solution(mesh):
    return jax.shard_map(
        per_device,
        mesh=mesh,
        in_specs=(
            P("group", ("row", "col")),
            P("row", "col"),
            P("row", "col"),
            P("group", ("row", "col"), None),
            P("group", None, "col", "row", None),
            P("group"),
            P(),
        ),
        out_specs=P("group", "col", "row", None),
        check_vma=False,
    )
```

```python
import functools

import jax
import jax.numpy as jnp
from jax import lax
from jax.experimental import pallas as pl
from jax.experimental.pallas import tpu as pltpu
from jax.sharding import PartitionSpec as P

MESH = pl.DeviceIdType.MESH
F32 = jnp.float32
BF16 = jnp.bfloat16
I32 = jnp.int32

NX = 4
NZ = 12
NROW = 8
NFLAT = 16
ROWS = 256
FEAT = 512
BLK = 48
RANK = 64
AD = 4
SLAB_W = NX * AD * RANK

CHUNKS = ((0, 1), (2, 3), (4, 5))


def kernel(
    act_h,
    codes_h,
    scl_h,
    down_h,
    up_h,
    ids_ref,
    tab_ref,
    out_ref,
    a_all,
    w_v,
    scl_v,
    down_v,
    up_v,
    tab_v,
    choose,
    xs,
    xr,
    ids_s,
    ids_r,
    d_all,
    u_all,
    part,
    sp,
    sm,
    rp,
    rm,
    low_s,
    red,
    low_full,
    back_s,
    back_r,
    acc,
    load_sem,
    w_sem,
    a_sem,
    x_send,
    x_recv,
    i_send,
    i_recv,
    ad_send,
    ad_recv,
    rs_send,
    rs_recv,
    low_send,
    red_recv,
    full_send,
    full_recv,
    b_send,
    b_recv,
    hello,
):
    g = lax.axis_index("group")
    r = lax.axis_index("row")
    c = lax.axis_index("col")
    x = g // NZ
    z = g % NZ
    flat = 2 * r + c

    def at_z(there):
        return (x * NZ + there, r, c)

    def at_x(offset):
        return (((x + offset + NX) % NX) * NZ + z, r, c)

    def at_row(offset):
        return (g, (r + offset + NROW) % NROW, c)

    def block_of(i):
        return (r + 4 + ((i + 1) // 2) * (1 - 2 * (i % 2)) + NROW) % NROW

    load_a = pltpu.make_async_copy(act_h, a_all.at[c], load_sem.at[0])
    load_s = pltpu.make_async_copy(scl_h, scl_v, load_sem.at[1])
    load_d = pltpu.make_async_copy(down_h, down_v, load_sem.at[2])
    load_u = pltpu.make_async_copy(up_h, up_v, load_sem.at[3])

    def load_w(i):
        columns = pl.ds(pl.multiple_of(block_of(i) * FEAT, FEAT), FEAT)
        return pltpu.make_async_copy(codes_h.at[:, columns], w_v.at[i], w_sem.at[i])

    load_a.start()
    load_d.start()
    load_u.start()
    load_w(0).start()
    load_s.start()
    for i in range(1, NROW):
        load_w(i).start()

    barrier = pltpu.get_barrier_semaphore()
    for o in range(1, NX):
        pl.semaphore_signal(barrier, inc=1, device_id=at_x(o), device_id_type=MESH)

    def greet_later(there, carry):
        pl.semaphore_signal(barrier, inc=1, device_id=at_z(there), device_id_type=MESH)
        return carry

    def greet(i, carry):
        pl.semaphore_signal(
            barrier,
            inc=1,
            device_id=(g, (r + i // 2) % NROW, (c + i % 2) % 2),
            device_id_type=MESH,
        )
        return carry

    lax.fori_loop(1, NFLAT, greet, 0)
    lax.fori_loop(z + 1, NZ, greet_later, 0)

    pl.semaphore_wait(barrier, NX - 1 + NFLAT - 1 + z)

    def greet_earlier(there, carry):
        pl.semaphore_signal(hello.at[z], inc=1, device_id=at_z(there), device_id_type=MESH)
        return carry

    lax.fori_loop(0, z, greet_earlier, 0)

    tab_v[...] = jnp.zeros(tab_v.shape, F32)
    tab_v[:, : tab_ref.shape[1]] = tab_ref[...].astype(F32)
    ids = ids_ref[...]
    match = (lax.broadcasted_iota(I32, (256, ROWS), 0) == ids).astype(F32).astype(BF16)
    slots = jnp.dot(
        jnp.broadcast_to(tab_v[...], (8, 256)).astype(BF16), match, preferred_element_type=F32
    ).astype(I32)
    owner = slots >> 2
    owner_x = (
        (owner >= NZ).astype(I32) + (owner >= 2 * NZ).astype(I32) + (owner >= 3 * NZ).astype(I32)
    )
    place = owner - NZ * owner_x
    adapter = (owner_x * AD + (slots & 3) + 1).astype(F32).astype(BF16)
    sent_to = lax.broadcasted_iota(I32, (16, ROWS), 0) == place[0:1]
    before = (
        lax.broadcasted_iota(I32, (ROWS, ROWS), 0) < lax.broadcasted_iota(I32, (ROWS, ROWS), 1)
    )
    prefix = jnp.dot(
        sent_to.astype(F32).astype(BF16),
        before.astype(F32).astype(BF16),
        preferred_element_type=F32,
    )
    position = jnp.sum(jnp.where(sent_to, prefix, 0.0), axis=0, keepdims=True).astype(I32)
    target = place[0:1] * BLK + position

    swap_a = pltpu.make_async_remote_copy(
        src_ref=a_all.at[c],
        dst_ref=a_all.at[c],
        send_sem=a_sem.at[0],
        recv_sem=a_sem.at[1],
        device_id=(g, r, 1 - c),
        device_id_type=MESH,
    )
    take_a = pltpu.make_async_remote_copy(
        src_ref=a_all.at[1 - c],
        dst_ref=a_all.at[1 - c],
        send_sem=a_sem.at[0],
        recv_sem=a_sem.at[1],
        device_id=(g, r, 1 - c),
        device_id_type=MESH,
    )

    def share(buffer, base, step):
        return pltpu.make_async_remote_copy(
            src_ref=buffer.at[x],
            dst_ref=buffer.at[x],
            send_sem=ad_send.at[base + step],
            recv_sem=ad_recv.at[base + step],
            device_id=at_x(step),
            device_id_type=MESH,
        )

    def arrived(buffer, base, step):
        return pltpu.make_async_remote_copy(
            src_ref=buffer.at[(x + NX - step) % NX],
            dst_ref=buffer.at[(x + NX - step) % NX],
            send_sem=ad_send.at[base + step],
            recv_sem=ad_recv.at[base + step],
            device_id=at_x(step),
            device_id_type=MESH,
        )

    load_d.wait()
    d_all[x] = down_v[...].astype(BF16)
    for step in (2, 1, 3):
        share(d_all, 0, step).start()
    load_a.wait()
    swap_a.start()

    choose[...] = (
        (lax.broadcasted_iota(I32, (NZ * BLK, ROWS), 0) == target).astype(F32).astype(BF16)
    )
    ids_s[...] = jnp.zeros(ids_s.shape, F32)
    for q in range(NZ):
        row = lax.dot_general(
            adapter,
            choose[q * BLK : (q + 1) * BLK, :],
            (((1,), (1,)), ((), ())),
            preferred_element_type=F32,
        )
        ids_s[q, :, 0:BLK] = row[0:1]
    ids_r[z] = ids_s[z]
    xs[...] = (
        jnp.dot(choose[...], a_all[c], preferred_element_type=F32)
        .astype(BF16)
        .reshape(NZ, BLK, FEAT)
    )
    xr[z] = xs[z]

    def send_rows(there):
        return pltpu.make_async_remote_copy(
            src_ref=xs.at[there],
            dst_ref=xr.at[z],
            send_sem=x_send.at[there],
            recv_sem=x_recv.at[z],
            device_id=at_z(there),
            device_id_type=MESH,
        )

    def take_rows(there):
        return pltpu.make_async_remote_copy(
            src_ref=xr.at[there],
            dst_ref=xr.at[there],
            send_sem=x_send.at[there],
            recv_sem=x_recv.at[there],
            device_id=at_z(there),
            device_id_type=MESH,
        )

    def send_ids(there):
        return pltpu.make_async_remote_copy(
            src_ref=ids_s.at[there],
            dst_ref=ids_r.at[z],
            send_sem=i_send.at[there],
            recv_sem=i_recv.at[z],
            device_id=at_z(there),
            device_id_type=MESH,
        )

    def take_ids(there):
        return pltpu.make_async_remote_copy(
            src_ref=ids_r.at[there],
            dst_ref=ids_r.at[there],
            send_sem=i_send.at[there],
            recv_sem=i_recv.at[there],
            device_id=at_z(there),
            device_id_type=MESH,
        )

    def send_back(there):
        return pltpu.make_async_remote_copy(
            src_ref=back_s.at[there],
            dst_ref=back_r.at[z],
            send_sem=b_send.at[there],
            recv_sem=b_recv.at[z],
            device_id=at_z(there),
            device_id_type=MESH,
        )

    def take_back(there):
        return pltpu.make_async_remote_copy(
            src_ref=back_r.at[there],
            dst_ref=back_r.at[there],
            send_sem=b_send.at[there],
            recv_sem=b_recv.at[there],
            device_id=at_z(there),
            device_id_type=MESH,
        )

    def post_earlier(k, carry):
        there = jnp.where(k % 2 == 0, k // 2, z - 1 - k // 2)
        send_ids(there).start()
        send_rows(there).start()
        return carry

    lax.fori_loop(0, z, post_earlier, 0)

    def post_later(there):
        @pl.when(there < NZ)
        def _():
            pl.semaphore_wait(hello.at[there], 1)
            send_ids(there).start()
            send_rows(there).start()

    load_u.wait()
    for q in range(FEAT // 128):
        u_all[x, :, q * 128 : (q + 1) * 128] = up_v[pl.ds(q, AD * RANK, stride=4), :].astype(BF16)
    for step in (2, 1, 3):
        share(u_all, 4, step).start()

    half_rows = (pl.ds(0, ROWS // 2), pl.ds(ROWS // 2, ROWS // 2))

    def ring(direction, step, half):
        source, landing, way = ((sp, rp, 1), (sm, rm, -1))[direction]
        return pltpu.make_async_remote_copy(
            src_ref=source.at[step, half_rows[half]],
            dst_ref=landing.at[step, half_rows[half]],
            send_sem=rs_send.at[direction, step, half],
            recv_sem=rs_recv.at[direction, step, half],
            device_id=at_row(way),
            device_id_type=MESH,
        )

    load_s.wait()
    take_a.wait_recv()

    def base_block(i, carry):
        load_w(i).wait()
        columns = pl.ds(pl.multiple_of(block_of(i) * FEAT, FEAT), FEAT)
        scale = jnp.exp2(scl_v[:, columns].astype(F32)).astype(BF16)
        weight = (w_v[i].reshape(32, 32, FEAT) * scale[:, None, :]).reshape(2 * FEAT, FEAT)
        value = jnp.dot(a_all[0], weight[:FEAT], preferred_element_type=F32)
        value += jnp.dot(a_all[1], weight[FEAT:], preferred_element_type=F32)
        part[i] = value

        @pl.when(i == 0)
        def _():
            sp[0, half_rows[0]] = part[0, half_rows[0]].astype(BF16)
            ring(0, 0, 0).start()
            sm[0, half_rows[1]] = part[0, half_rows[1]].astype(BF16)
            ring(1, 0, 1).start()

        @pl.when(i == 1)
        def _():
            sp[1, half_rows[1]] = part[1, half_rows[1]].astype(BF16)
            ring(0, 1, 1).start()

        @pl.when(i == 2)
        def _():
            sm[1, half_rows[0]] = part[2, half_rows[0]].astype(BF16)
            ring(1, 1, 0).start()

        post_later(z + 1 + i)
        return carry

    lax.fori_loop(0, NROW, base_block, 0)
    for later in range(NROW + 1, NZ):
        post_later(z + later)

    def ring_step(direction, step, half):
        ring(direction, step - 1, half).wait_recv()
        source, landing, _ = ((sp, rp, 1), (sm, rm, -1))[direction]
        rows = half_rows[half]
        own = part[2 * step - 1 + direction, rows]
        source[step, rows] = (landing[step - 1, rows].astype(F32) + own).astype(BF16)
        ring(direction, step, half).start()

    lane = lax.broadcasted_iota(I32, (BLK // 2, 128), 1)
    eye = lax.broadcasted_iota(I32, (BLK, 128), 0) == lax.broadcasted_iota(I32, (BLK, 128), 1)
    lane_adapter = (lax.broadcasted_iota(I32, (BLK, SLAB_W), 1) // RANK + 1).astype(F32)

    def adapter_mask(q):
        wanted = jnp.sum(jnp.where(eye, ids_r[q], 0.0), axis=1, keepdims=True)
        return lane_adapter == wanted

    def reducer(p):
        return (3 * p) % NROW, p % 2

    def adds_up(p):
        row, col = reducer(p)
        return flat == 2 * row + col

    def to_reducer(p):
        row, col = reducer(p)
        return pltpu.make_async_remote_copy(
            src_ref=low_s.at[p],
            dst_ref=red.at[flat],
            send_sem=low_send.at[p],
            recv_sem=red_recv.at[flat],
            device_id=(g, row, col),
            device_id_type=MESH,
        )

    def from_device(i):
        return pltpu.make_async_remote_copy(
            src_ref=red.at[i],
            dst_ref=red.at[i],
            send_sem=low_send.at[0],
            recv_sem=red_recv.at[i],
            device_id=(g, (r + 1) % NROW, c),
            device_id_type=MESH,
        )

    def to_all(p, i):
        return pltpu.make_async_remote_copy(
            src_ref=low_full.at[p],
            dst_ref=low_full.at[p],
            send_sem=full_send.at[i],
            recv_sem=full_recv.at[p],
            device_id=(g, (r + i // 2) % NROW, (c + i % 2) % 2),
            device_id_type=MESH,
        )

    def sources(chunk):
        return [2 * p + k for p in chunk for k in (0, 1)]

    def project(chunk):
        for q in sources(chunk):

            @pl.when(z != q)
            def _():
                take_ids(q).wait_recv()
                take_rows(q).wait_recv()

        projected = lax.dot_general(
            jnp.concatenate([xr[q] for q in sources(chunk)], axis=0),
            d_all[...].reshape(SLAB_W, FEAT),
            (((1,), (1,)), ((), ())),
            preferred_element_type=F32,
        )
        for n, p in enumerate(chunk):
            halves = []
            for k, q in enumerate((2 * p, 2 * p + 1)):
                block = projected[(2 * n + k) * BLK : (2 * n + k + 1) * BLK]
                block = jnp.where(adapter_mask(q), block, 0.0)
                folded = block[:, 0:128]
                for m in range(1, SLAB_W // 128):
                    folded += block[:, m * 128 : (m + 1) * 128]
                folded += pltpu.roll(folded, RANK, 1)
                halves.append(jnp.where(lane < RANK, folded[: BLK // 2], folded[BLK // 2 :]))
            low_s[p] = jnp.concatenate(halves, axis=0).astype(BF16)

            @pl.when(jnp.logical_not(adds_up(p)))
            def _():
                to_reducer(p).start()

            @pl.when(adds_up(p))
            def _():
                red[flat] = low_s[p]

    def reduce_low(chunk):
        for p in chunk:

            @pl.when(adds_up(p))
            def _():
                row, col = reducer(p)
                for i in range(NFLAT):
                    if i != 2 * row + col:
                        from_device(i).wait_recv()
                total = red[0].astype(F32)
                for i in range(1, NFLAT):
                    total += red[i].astype(F32)
                low_full[p] = total.astype(BF16)

                def hand_out(i, carry):
                    to_all(p, i).start()
                    return carry

                lax.fori_loop(1, NFLAT, hand_out, 0)

    def expand(chunk):
        spread = []
        for p in chunk:

            @pl.when(jnp.logical_not(adds_up(p)))
            def _():
                to_all(p, 1).wait_recv()

            summed = low_full[p].astype(F32)
            for q in (2 * p, 2 * p + 1):
                packed = summed[(q % 2) * (BLK // 2) : (q % 2 + 1) * (BLK // 2)]
                turned = pltpu.roll(packed, RANK, 1)
                both = jnp.concatenate(
                    [
                        jnp.where(lane < RANK, packed, turned),
                        jnp.where(lane < RANK, turned, packed),
                    ],
                    axis=0,
                )
                wide = jnp.concatenate([both] * (SLAB_W // 128), axis=1)
                spread.append(jnp.where(adapter_mask(q), wide, 0.0).astype(BF16))
        delta = jnp.dot(
            jnp.concatenate(spread, axis=0),
            u_all[...].reshape(SLAB_W, FEAT),
            preferred_element_type=F32,
        ).astype(BF16)
        for n, q in enumerate(sources(chunk)):
            back_s[q] = delta[n * BLK : (n + 1) * BLK]

            @pl.when(z != q)
            def _():
                send_back(q).start()

            @pl.when(z == q)
            def _():
                back_r[q] = back_s[q]

    ring_step(0, 1, 0)
    ring_step(1, 1, 1)
    for step in range(1, NX):
        arrived(d_all, 0, step).wait_recv()
    project(CHUNKS[0])
    ring_step(0, 2, 1)
    ring_step(1, 2, 0)
    reduce_low(CHUNKS[0])
    ring_step(0, 2, 0)
    ring_step(1, 2, 1)
    project(CHUNKS[1])
    for step in range(1, NX):
        arrived(u_all, 4, step).wait_recv()
    expand(CHUNKS[0])
    reduce_low(CHUNKS[1])
    project(CHUNKS[2])
    expand(CHUNKS[1])
    reduce_low(CHUNKS[2])
    ring_step(0, 3, 1)
    ring_step(1, 3, 0)
    ring_step(0, 3, 0)
    ring_step(1, 3, 1)
    expand(CHUNKS[2])

    for half in (1, 0):
        ring(0, 3, half).wait_recv()
        ring(1, 3, 1 - half).wait_recv()
    acc[...] = part[7] + (rp[3].astype(F32) + rm[3].astype(F32))

    for q in range(NZ):

        @pl.when(z != q)
        def _():
            take_back(q).wait_recv()

    added = lax.dot_general(
        choose[...],
        back_r[...].reshape(NZ * BLK, FEAT),
        (((0,), (0,)), ((), ())),
        preferred_element_type=F32,
    )
    out_ref[...] = (acc[...] + added).astype(BF16)

    swap_a.wait_send()
    for q in range(NZ):

        @pl.when(z != q)
        def _():
            send_ids(q).wait_send()
            send_rows(q).wait_send()
            send_back(q).wait_send()

    for buffer, base in ((d_all, 0), (u_all, 4)):
        for step in range(1, NX):
            share(buffer, base, step).wait_send()
    for direction in (0, 1):
        ring(direction, 0, direction).wait_send()
        for step in (1, 2, 3):
            for half in (0, 1):
                ring(direction, step, half).wait_send()
    for p in range(NZ // 2):

        @pl.when(jnp.logical_not(adds_up(p)))
        def _():
            to_reducer(p).wait_send()

        @pl.when(adds_up(p))
        def _():
            def left(i, carry):
                to_all(p, i).wait_send()
                return carry

            lax.fori_loop(1, NFLAT, left, 0)


def per_device(
    activations,
    base_weight_codes,
    block_scale_exponents,
    adapter_down_weight,
    adapter_up_weight,
    row_adapter_index,
    adapter_storage_slot,
):
    down = jnp.transpose(adapter_down_weight, (0, 2, 1)).reshape(AD * RANK, FEAT)
    up = adapter_up_weight.reshape(AD * RANK * FEAT // 128, 128)
    hbm = pl.BlockSpec(memory_space=pl.ANY)
    vmem = pl.BlockSpec(memory_space=pltpu.VMEM)
    dma = pltpu.SemaphoreType.DMA
    padded = NZ * BLK
    out = pl.pallas_call(
        kernel,
        out_shape=jax.ShapeDtypeStruct((ROWS, FEAT), BF16),
        in_specs=[hbm] * 5 + [vmem] * 2,
        out_specs=vmem,
        scratch_shapes=[
            pltpu.VMEM((2, ROWS, FEAT), BF16),
            pltpu.VMEM((NROW, 2 * FEAT, FEAT), BF16),
            pltpu.VMEM((32, NROW * FEAT), I32),
            pltpu.VMEM((AD * RANK, FEAT), F32),
            pltpu.VMEM((AD * RANK * FEAT // 128, 128), F32),
            pltpu.VMEM((1, 256), F32),
            pltpu.VMEM((padded, ROWS), BF16),
            pltpu.VMEM((NZ, BLK, FEAT), BF16),
            pltpu.VMEM((NZ, BLK, FEAT), BF16),
            pltpu.VMEM((NZ, 1, 128), F32),
            pltpu.VMEM((NZ, 1, 128), F32),
            pltpu.VMEM((NX, AD * RANK, FEAT), BF16),
            pltpu.VMEM((NX, AD * RANK, FEAT), BF16),
            pltpu.VMEM((NROW, ROWS, FEAT), F32),
            pltpu.VMEM((4, ROWS, FEAT), BF16),
            pltpu.VMEM((4, ROWS, FEAT), BF16),
            pltpu.VMEM((4, ROWS, FEAT), BF16),
            pltpu.VMEM((4, ROWS, FEAT), BF16),
            pltpu.VMEM((NZ // 2, BLK, 128), BF16),
            pltpu.VMEM((NFLAT, BLK, 128), BF16),
            pltpu.VMEM((NZ // 2, BLK, 128), BF16),
            pltpu.VMEM((NZ, BLK, FEAT), BF16),
            pltpu.VMEM((NZ, BLK, FEAT), BF16),
            pltpu.VMEM((ROWS, FEAT), F32),
            dma((4,)),
            dma((NROW,)),
            dma((2,)),
            dma((NZ,)),
            dma((NZ,)),
            dma((NZ,)),
            dma((NZ,)),
            dma((8,)),
            dma((8,)),
            dma((2, 4, 2)),
            dma((2, 4, 2)),
            dma((NZ // 2,)),
            dma((NFLAT,)),
            dma((NFLAT,)),
            dma((NZ // 2,)),
            dma((NZ,)),
            dma((NZ,)),
            pltpu.SemaphoreType.REGULAR((NZ,)),
        ],
        compiler_params=pltpu.CompilerParams(
            collective_id=0, has_side_effects=True, vmem_limit_bytes=56 * 1024 * 1024
        ),
        cost_estimate=pl.CostEstimate(
            flops=2 * ROWS * 2 * FEAT * NROW * FEAT, bytes_accessed=11 << 20, transcendentals=0
        ),
        name="projection",
    )(
        activations,
        base_weight_codes,
        block_scale_exponents,
        down,
        up,
        row_adapter_index.reshape(1, ROWS),
        adapter_storage_slot.reshape(1, -1),
    )
    return out.reshape(ROWS, 1, 1, FEAT)


def solution(mesh):
    return jax.shard_map(
        per_device,
        mesh=mesh,
        in_specs=(
            P("group", ("row", "col")),
            P("row", "col"),
            P("row", "col"),
            P("group", ("row", "col"), None),
            P("group", None, "col", "row", None),
            P("group"),
            P(),
        ),
        out_specs=P("group", "col", "row", None),
        check_vma=False,
    )
```
